256 devices in a mesh: dp: 64 (over y, z, core), hidden: 4 (over x).
Axes of the slice: x: 4, y: 4, z: 8, core: 2. Of those that a mesh axis runs over, the one named last changes fastest.
Arguments:
- tokens: bfloat16 [32768, 8192], P('dp', 'hidden'), may hold values from -6 to 6
- qkv_weight: float32 [5120, 8192], P('dp', 'hidden'), may hold values from -24 to 24
- grad: float32 [5120, 8192], P('dp', 'hidden'), may hold values from -6 to 6
- adam_m: float32 [5120, 8192], P('dp', 'hidden'), may hold values from -2 to 2
- adam_v: float32 [5120, 8192], P('dp', 'hidden'), may hold values from 0.05 to 1
- head_gain: float32 [5120], P('hidden'), may hold values from 0.25 to 1.75
Outputs:
- new_weight: float32 [5120, 8192], P('dp', 'hidden')
- new_m: float32 [5120, 8192], P('dp', 'hidden')
- new_v: float32 [5120, 8192], P('dp', 'hidden')
- qkv: bfloat16 [32768, 5120], P('dp', 'hidden')
The draws below stay inside these ranges and needn't reach their ends.
All inputs are finite; a program needn't handle non-finite values.
Results may differ from the reference program's by a relative error of at most 0.015.
Values may be sent and summed in bfloat16 or wider, within the bound.
A program may use at most 192 MiB of HBM per device.

```python
import math
import jax
import jax.numpy as jnp
from jax import lax

D = 8192
HD = 128
TOK_DEV = 512
QR = 4096
KR = 512
ROWS = 5120
TOKENS = 32768
N_DP = 64
N_HIDDEN = 4


def ramp_factor(rise):
    ramp = jnp.arange(D, dtype=jnp.float32)[None, :] / D
    return jnp.exp((ramp - 0.5) * math.log(rise))


def draw_qkv_weight(key, part):
    key_base, key_rows, key_cols = jax.random.split(key, 3)
    base = jax.random.truncated_normal(key_base, -4.0, 4.0, (ROWS, D), jnp.float32)
    row_factor = jnp.exp(jax.random.uniform(key_rows, (ROWS, 1), jnp.float32, -0.2, 0.2))
    jitter = jnp.exp(jax.random.uniform(key_cols, (1, D), jnp.float32, -1.15, 1.15))
    col_factor = jitter * ramp_factor(3.0) / 1.617
    shifted = base
    return shifted * row_factor * col_factor


def shard_levels(key, extent, shards, low, high):
    def one(axis_at, parts):
        draws = jax.random.uniform(jax.random.fold_in(jax.random.fold_in(key, 6), axis_at), (parts,), jnp.float32, low / len(shards), high / len(shards))
        return jnp.repeat(jnp.exp(draws), extent[axis_at] // parts).reshape((-1,) + (1,) * (len(extent) - axis_at - 1))

    loudness = one(*shards[0])
    for cut in shards[1:]:
        loudness = loudness * one(*cut)
    return loudness


def gaussian(key, extent, spread, limit, cuts=(), kind=jnp.bfloat16):
    entries = jax.random.normal(key, extent, jnp.float32) * spread
    if len(cuts) > 0:
        entries = shard_levels(key, extent, cuts, -0.22, 0.18) * entries
    return jnp.clip(entries, min=-limit, max=limit).astype(kind)


def setup_inputs(seed: int = 0) -> dict:
    splits = jax.random.split(jax.random.key(seed), 7)
    return {
        "tokens": gaussian(splits[0], (TOKENS, D), 1.0, 6.0, ((0, 64), (1, 4))),
        "qkv_weight": draw_qkv_weight(jax.random.fold_in(splits[6], 71), 0),
        "grad": gaussian(splits[2], (ROWS, D), 1.0, 6.0, ((0, 64), (1, 4)), jnp.float32),
        "adam_m": gaussian(splits[3], (ROWS, D), 0.3, 2.0, ((0, 64), (1, 4)), jnp.float32),
        "adam_v": jnp.clip(jnp.exp(math.log(1.0) - 2.9957323 * jax.random.uniform(splits[4], (ROWS, D), jnp.float32) ** shard_levels(splits[4], (ROWS, D), ((0, 64), (1, 4)), -0.2, 0.2)), 0.05, 1.0),
        "head_gain": jnp.clip(1.0 + 0.15 * jax.random.normal(splits[5], (ROWS,), jnp.float32), 0.25, 1.75),
    }


beta_one = 0.9
beta_two = 0.95
learn_rate = 0.05
adam_eps = 1e-08
norm_eps = 1e-06
bias_one = 0.999973438601112
bias_two = 0.994079470779667

def reference(tokens, qkv_weight, grad, adam_m, adam_v, head_gain):
    new_m = beta_one * adam_m + (1.0 - beta_one) * grad
    new_v = beta_two * adam_v + (1.0 - beta_two) * grad * grad
    updated = qkv_weight - learn_rate * (new_m / bias_one) / (jnp.sqrt(new_v / bias_two) + adam_eps)
    row_scale = 1.0 / jnp.sqrt(lax.optimization_barrier(jnp.sum(updated * updated, axis=1)) / D + norm_eps)
    new_weight = updated * row_scale[:, None]
    weight_bf = updated.astype(jnp.bfloat16)
    width_shard = D // N_HIDDEN
    weight_slices = [weight_bf[:, group * width_shard:(group + 1) * width_shard].T for group in range(N_HIDDEN)]
    is_qk = (jnp.arange(ROWS // HD) < (QR + KR) // HD)[None, :, None]

    def project_block(token_block):
        total = jnp.zeros((TOK_DEV, ROWS), jnp.float32)
        for group in range(N_HIDDEN):
            token_slice = token_block[:, group * width_shard:(group + 1) * width_shard]
            piece = jnp.dot(token_slice, weight_slices[group], preferred_element_type=jnp.float32)
            total = total + lax.optimization_barrier(piece.astype(jnp.bfloat16)).astype(jnp.float32)
        proj = total * row_scale[None, :]
        heads = proj.reshape(TOK_DEV, ROWS // HD, HD)
        mean_sq = lax.optimization_barrier(jnp.mean(heads * heads, axis=2, keepdims=True))
        normed = heads / jnp.sqrt(mean_sq + norm_eps)
        plain = heads / math.sqrt(D)
        result = jnp.where(is_qk, normed, plain).reshape(TOK_DEV, ROWS) * head_gain[None, :]
        return result.astype(jnp.bfloat16)
    blocks = lax.map(project_block, tokens.reshape(N_DP, TOK_DEV, D))
    return (new_weight, new_m, new_v, blocks.reshape(TOKENS, ROWS))
```

```python
import math

import jax
import jax.numpy as jnp
from jax import lax
from jax.sharding import PartitionSpec as P

D = 8192
HD = 128
QR = 4096
KR = 512


beta_one = 0.9
beta_two = 0.95
learn_rate = 0.05
adam_eps = 1e-08
norm_eps = 1e-06
bias_one = 0.999973438601112
bias_two = 0.994079470779667


def body(tokens, qkv_weight, grad, adam_m, adam_v, head_gain):
    new_m = beta_one * adam_m + (1.0 - beta_one) * grad
    new_v = beta_two * adam_v + (1.0 - beta_two) * grad * grad
    updated = qkv_weight - learn_rate * (new_m / bias_one) / (jnp.sqrt(new_v / bias_two) + adam_eps)
    partial_value = jnp.sum(updated * updated, axis=1)
    weight_bf = updated.astype(jnp.bfloat16)
    row_total = lax.psum(partial_value, "hidden")
    row_scale = 1.0 / jnp.sqrt(row_total / D + norm_eps)
    new_weight = updated * row_scale[:, None]
    tok_rows = tokens.shape[0]
    local_cols = head_gain.shape[0]
    col_start = lax.axis_index("hidden") * local_cols
    gathered = lax.all_gather(weight_bf, "dp", axis=0, tiled=True)
    wide = gathered.astype(jnp.float32)
    col_total = lax.psum_scatter(
        jnp.sum(wide * wide, axis=1), "hidden", scatter_dimension=0, tiled=True
    )
    col_scale = 1.0 / jnp.sqrt(col_total / D + norm_eps)
    partial_proj = lax.dot_general(
        tokens,
        gathered,
        (((1,), (1,)), ((), ())),
        preferred_element_type=jnp.float32,
    )
    summed = lax.psum_scatter(
        partial_proj.astype(jnp.bfloat16), "hidden", scatter_dimension=1, tiled=True
    ).astype(jnp.float32)
    proj = summed * col_scale[None, :]
    heads = proj.reshape(tok_rows, local_cols // HD, HD)
    mean_sq = jnp.mean(heads * heads, axis=2, keepdims=True)
    normed = heads / jnp.sqrt(mean_sq + norm_eps)
    plain = heads / math.sqrt(D)
    head_index = col_start // HD + jnp.arange(local_cols // HD, dtype=jnp.int32)
    is_qk = (head_index < (QR + KR) // HD)[None, :, None]
    result = jnp.where(is_qk, normed, plain).reshape(tok_rows, local_cols) * head_gain[None, :]
    return (new_weight, new_m, new_v, result.astype(jnp.bfloat16))


def solution(mesh):
    return jax.shard_map(
        body,
        mesh=mesh,
        in_specs=(
            P("dp", "hidden"),
            P("dp", "hidden"),
            P("dp", "hidden"),
            P("dp", "hidden"),
            P("dp", "hidden"),
            P("hidden"),
        ),
        out_specs=(P("dp", "hidden"), P("dp", "hidden"), P("dp", "hidden"), P("dp", "hidden")),
        check_vma=False,
    )
```

```python
import math

import jax
import jax.numpy as jnp
from jax import lax
from jax.experimental import pallas as pl
from jax.experimental.pallas import tpu as pltpu
from jax.sharding import PartitionSpec as P

D = 8192
HD = 128
QR = 4096
KR = 512

NY, NZ, NX = 4, 8, 4
ROWS = 80
SPLIT = 32
KS = 2048
TOK = 512
COLS = 1280
HALF = KS // 2

beta_one = 0.9
beta_two = 0.95
learn_rate = 0.05
adam_eps = 1e-08
norm_eps = 1e-06
bias_one = 0.999973438601112
bias_two = 0.994079470779667

MESH = pl.DeviceIdType.MESH
SIGNS = (1, -1)


def side(s):
    return 0 if s > 0 else 1


def group_of(dz):
    if dz == 0:
        return 0
    if dz == 4:
        return 7
    return 2 * dz - 1 if dz > 0 else -2 * dz


def kernel(
    tok, upd, gain, out, scale_out,
    wbuf, tokbuf, pbuf, inc, rel, fin, sq,
    s_ay, r_ay, s_az, r_az, s_bz, r_bz, s_by, r_by,
    s_x, r_inc, r_fin, r_sib, s_sq, r_sq, tok_sem,
):
    dp = lax.axis_index("dp")
    x = lax.axis_index("hidden")
    y = lax.div(dp, 16)
    z = lax.rem(lax.div(dp, 2), NZ)
    c = lax.rem(dp, 2)

    def device(dy=0, dz=0, dx=0, core=None):
        yy = lax.rem(y + dy + NY, NY)
        zz = lax.rem(z + dz + NZ, NZ)
        return ((yy * NZ + zz) * 2 + (c if core is None else core), lax.rem(x + dx + NX, NX))

    def at_y(dy):
        return lax.rem(y + dy + NY, NY)

    def at_z(dz):
        return lax.rem(z + dz + NZ, NZ)

    def at_x(dx):
        return lax.rem(x + dx + NX, NX)

    y_dev = {s: device(dy=s) for s in SIGNS}
    z_dev = {s: device(dz=s) for s in SIGNS}
    x_dev = {(s, k): device(dx=s, core=k) for s in SIGNS for k in (0, 1)}
    x_two = device(dx=2)
    sibling = device(core=1 - c)

    barrier = pltpu.get_barrier_semaphore()
    partners = list(y_dev.values()) + list(z_dev.values()) + list(x_dev.values()) + [x_two, sibling]
    for partner in partners:
        pl.semaphore_signal(barrier, inc=1, device_id=partner, device_id_type=MESH)

    def copy(src, dst, send_sem, recv_sem, dev):
        return pltpu.make_async_remote_copy(
            src_ref=src, dst_ref=dst, send_sem=send_sem, recv_sem=recv_sem,
            device_id=dev, device_id_type=MESH,
        )

    own_tok = pltpu.make_async_copy(tok, tokbuf.at[c], tok_sem.at[0])
    own_tok.start()

    updated = upd[...]
    squares = updated * updated
    part = squares[:, 0:128]
    for i in range(1, KS // 128):
        part = part + squares[:, i * 128:(i + 1) * 128]
    sq[x] = part

    pl.semaphore_wait(barrier, len(partners))

    sq_dev = {1: device(dx=1), 2: x_two, 3: device(dx=3)}
    sq_out = [copy(sq.at[x], sq.at[x], s_sq.at[d - 1], r_sq.at[d - 1], sq_dev[d]) for d in (1, 2, 3)]
    for d in (1, 0, 2):
        sq_out[d].start()
    tok_out = copy(tok, tokbuf.at[c], tok_sem.at[1], tok_sem.at[2], sibling)
    tok_out.start()
    for d in (1, 2, 3):
        slot = sq.at[at_x(-d)]
        copy(slot, slot, s_sq.at[d - 1], r_sq.at[d - 1], sibling).wait_recv()
    total = jnp.sum(sq[0] + sq[1] + sq[2] + sq[3], axis=1, keepdims=True)
    row_scale = 1.0 / jnp.sqrt(total / D + norm_eps)
    scale_out[...] = jnp.broadcast_to(row_scale, (ROWS, 128))
    wbuf[z, y] = (updated * row_scale).astype(jnp.bfloat16)

    def part_a(zz, yy, s=None):
        ref = wbuf.at[zz, yy, pl.ds(0, SPLIT)]
        return ref if s is None else ref.at[:, pl.ds(side(s) * HALF, HALF)]

    def part_b(zz, yy, s=None):
        ref = wbuf.at[zz, yy, pl.ds(SPLIT, ROWS - SPLIT)]
        return ref if s is None else ref.at[:, pl.ds(side(s) * HALF, HALF)]

    y_order = (0, -1, 1, 2)

    def ay(hop, s):
        if hop == 1:
            ref = part_a(z, y)
        else:
            ref = part_a(z, at_y(-s), s)
        return copy(ref, ref, s_ay.at[hop - 1, side(s)], r_ay.at[hop - 1, side(s)], y_dev[s])

    def ay_recv(hop, s):
        ref = part_a(z, at_y(-s)) if hop == 1 else part_a(z, at_y(-2 * s), s)
        copy(ref, ref, s_ay.at[hop - 1, side(s)], r_ay.at[hop - 1, side(s)], y_dev[s]).wait_recv()

    def az(k, s, j):
        ref = part_a(at_z(-(k - 1) * s), at_y(y_order[j]), s if k == 4 else None)
        return copy(ref, ref, s_az.at[k - 1, side(s), j], r_az.at[k - 1, side(s), j], z_dev[s])

    def az_recv(k, s, j):
        ref = part_a(at_z(-k * s), at_y(y_order[j]), s if k == 4 else None)
        copy(ref, ref, s_az.at[k - 1, side(s), j], r_az.at[k - 1, side(s), j], z_dev[s]).wait_recv()

    def bz(k, s):
        ref = part_b(at_z(-(k - 1) * s), y, s if k == 4 else None)
        return copy(ref, ref, s_bz.at[k - 1, side(s)], r_bz.at[k - 1, side(s)], z_dev[s])

    def bz_recv(k, s):
        ref = part_b(at_z(-k * s), y, s if k == 4 else None)
        copy(ref, ref, s_bz.at[k - 1, side(s)], r_bz.at[k - 1, side(s)], z_dev[s]).wait_recv()

    def by(dz, hop, s):
        g = group_of(dz)
        ref = part_b(at_z(-dz), y) if hop == 1 else part_b(at_z(-dz), at_y(-s), s)
        return copy(ref, ref, s_by.at[g, hop - 1, side(s)], r_by.at[g, hop - 1, side(s)], y_dev[s])

    def by_recv(dz, hop, s):
        g = group_of(dz)
        ref = part_b(at_z(-dz), at_y(-s)) if hop == 1 else part_b(at_z(-dz), at_y(-2 * s), s)
        copy(ref, ref, s_by.at[g, hop - 1, side(s)], r_by.at[g, hop - 1, side(s)], y_dev[s]).wait_recv()

    for s in SIGNS:
        ay(1, s).start()
        bz(1, s).start()
    for s in SIGNS:
        by(0, 1, s).start()
        az(1, s, 0).start()

    def widen(k):
        for s in SIGNS:
            for j in range(4):
                az_recv(k, s, j)
                az(k + 1, s, j).start()
        widen_b(k + 1)
        for dz in (k, -k):
            for s in SIGNS:
                by_recv(dz, 1, s)
                by(dz, 2, s).start()

    def widen_b(k):
        if k < 4:
            for s in SIGNS:
                bz_recv(k, s)
                bz(k + 1, s).start()
                for t in SIGNS:
                    by(k * s, 1, t).start()
        else:
            for s in SIGNS:
                bz_recv(k, s)
            for t in SIGNS:
                by(4, 1, t).start()

    def arrive(dz):
        for s in SIGNS:
            by_recv(dz, 2, s)

    def step_0():
        for s in SIGNS:
            ay_recv(1, s)
            ay(2, s).start()
        for j in (1, 2):
            for s in SIGNS:
                az(1, s, j).start()
        widen_b(1)
        for s in SIGNS:
            by_recv(0, 1, s)
            by(0, 2, s).start()
        for s in SIGNS:
            ay_recv(2, s)
        for s in SIGNS:
            az(1, s, 3).start()
        arrive(0)

    def step_odd(k):
        def run():
            widen(k)
            arrive(k)
        return run

    def step_even(k):
        return lambda: arrive(-k)

    def step_7():
        for s in SIGNS:
            for j in range(4):
                az_recv(4, s, j)
            by_recv(4, 1, s)
            by(4, 2, s).start()
        arrive(4)

    steps = [step_0, step_odd(1), step_even(1), step_odd(2), step_even(2), step_odd(3), step_even(3), step_7]

    own_tok.wait()
    copy(tok, tokbuf.at[1 - c], tok_sem.at[1], tok_sem.at[2], sibling).wait_recv()

    def z_of(g):
        dz = jnp.where(lax.rem(g, 2) == 1, lax.div(g + 1, 2), -lax.div(g, 2))
        return lax.rem(z - dz + NZ, NZ)

    def place(zz, core):
        return pl.ds(pl.multiple_of(zz * (2 * ROWS) + core * ROWS, 16), ROWS)

    def send(g, i):
        zz = z_of(g)
        here = place(zz, c)
        fin_sem = lambda k: r_fin.at[k, zz, c]
        src, dst, recv_sem, dev = (
            lambda: (pbuf.at[g, at_x(2), 0], inc.at[g, 0], r_inc.at[g, 0], device(dx=-1)),
            lambda: (pbuf.at[g, at_x(2), 1], inc.at[g, 1], r_inc.at[g, 1], device(dx=1)),
            lambda: (pbuf.at[g, at_x(-1), 1], fin.at[0, here], fin_sem(0), x_dev[-1, 1]),
            lambda: (pbuf.at[g, at_x(1), 0], fin.at[1, here], fin_sem(1), x_dev[1, 0]),
            lambda: (pbuf.at[g, x, 1 - c], fin.at[2, here], r_sib.at[zz], sibling),
            lambda: (rel.at[g, 0], fin.at[0, here], fin_sem(0), x_dev[-1, 0]),
            lambda: (rel.at[g, 1], fin.at[1, here], fin_sem(1), x_dev[1, 1]),
        )[i]()
        return copy(src, dst, s_x.at[g, i], recv_sem, dev)

    def relay(g):
        for i, owner in ((0, at_x(-1)), (1, at_x(1))):
            send(g, i).wait_recv()
            mixed = pbuf[g, owner, i].astype(jnp.float32) + inc[g, i].astype(jnp.float32)
            rel[g, i] = mixed.astype(jnp.bfloat16)
            send(g, 5 + i).start()

    @pl.loop(0, 8)
    def _(g):
        for i, step in enumerate(steps):
            pl.when(g == i)(step)
        zz = z_of(g)

        @pl.loop(0, 4)
        def _(t):
            half = lax.div(t, 2)
            lanes = pl.ds(pl.multiple_of(lax.rem(t, 2) * 256, 256), 256)
            product = lax.dot_general(
                wbuf[zz].reshape(NY * ROWS, KS),
                tokbuf[half, lanes, :],
                (((1,), (1,)), ((), ())),
                preferred_element_type=jnp.float32,
            )
            pbuf[g, :, half, :, lanes] = product.reshape(NY, ROWS, 256).astype(jnp.bfloat16)

        for i in range(5):
            send(g, i).start()
        fin[2, place(zz, c)] = pbuf[g, x, c]

        @pl.when(g > 0)
        def _():
            relay(g - 1)

    relay(7)

    for zz in range(NZ):
        for core in (0, 1):
            for i in (0, 1):
                slot = fin.at[i, place(zz, core)]
                copy(slot, slot, s_x.at[0, 0], r_fin.at[i, zz, core], sibling).wait_recv()
        slot = fin.at[2, place(zz, 1 - c)]
        copy(slot, slot, s_x.at[0, 0], r_sib.at[zz], sibling).wait_recv()

    @pl.loop(0, COLS // HD)
    def _(h):
        rows = pl.ds(pl.multiple_of(h * HD, HD), HD)
        proj = (fin[0, rows].astype(jnp.float32) + fin[1, rows].astype(jnp.float32)) + fin[2, rows].astype(jnp.float32)
        mean_sq = jnp.sum(proj * proj, axis=0, keepdims=True) / HD
        is_qk = x * (COLS // HD) + h < (QR + KR) // HD
        factor = jnp.where(is_qk, 1.0 / jnp.sqrt(mean_sq + norm_eps), 1.0 / math.sqrt(D))
        out[:, rows] = ((proj * factor).T * gain[h]).astype(jnp.bfloat16)

    for sq_send in sq_out:
        sq_send.wait_send()
    tok_out.wait_send()
    for s in SIGNS:
        for hop in (1, 2):
            ay(hop, s).wait_send()
        for k in range(1, 5):
            bz(k, s).wait_send()
            for j in range(4):
                az(k, s, j).wait_send()
        for dz in (0, 1, -1, 2, -2, 3, -3, 4):
            for hop in (1, 2):
                by(dz, hop, s).wait_send()

    @pl.loop(0, 8)
    def _(g):
        for i in range(7):
            send(g, i).wait_send()


def project(tokens, updated, head_gain):
    dma = pltpu.SemaphoreType.DMA
    vmem = pl.BlockSpec(memory_space=pltpu.VMEM)
    bf16 = jnp.bfloat16
    return pl.pallas_call(
        kernel,
        out_shape=(
            jax.ShapeDtypeStruct((TOK, COLS), bf16),
            jax.ShapeDtypeStruct((ROWS, 128), jnp.float32),
        ),
        in_specs=[pl.BlockSpec(memory_space=pl.ANY), vmem, vmem],
        out_specs=(vmem, vmem),
        scratch_shapes=[
            pltpu.VMEM((NZ, NY, ROWS, KS), bf16),
            pltpu.VMEM((2, TOK, KS), bf16),
            pltpu.VMEM((8, NX, 2, ROWS, TOK), bf16),
            pltpu.VMEM((8, 2, ROWS, TOK), bf16),
            pltpu.VMEM((8, 2, ROWS, TOK), bf16),
            pltpu.VMEM((3, COLS, TOK), bf16),
            pltpu.VMEM((NX, ROWS, 128), jnp.float32),
            dma((2, 2)), dma((2, 2)),
            dma((4, 2, 4)), dma((4, 2, 4)),
            dma((4, 2)), dma((4, 2)),
            dma((8, 2, 2)), dma((8, 2, 2)),
            dma((8, 7)), dma((8, 2)), dma((2, NZ, 2)), dma((NZ,)),
            dma((3,)), dma((3,)), dma((3,)),
        ],
        compiler_params=pltpu.CompilerParams(
            collective_id=0, has_side_effects=True, vmem_limit_bytes=48 * 2**20
        ),
        cost_estimate=pl.CostEstimate(
            flops=2 * 2 * TOK * KS * NZ * NY * ROWS, bytes_accessed=4 * 2**20, transcendentals=0
        ),
    )(tokens, updated, head_gain.reshape(COLS // HD, 1, HD))


def body(tokens, qkv_weight, grad, adam_m, adam_v, head_gain):
    new_m = beta_one * adam_m + (1.0 - beta_one) * grad
    new_v = beta_two * adam_v + (1.0 - beta_two) * grad * grad
    updated = qkv_weight - learn_rate * (new_m / bias_one) / (jnp.sqrt(new_v / bias_two) + adam_eps)
    qkv, row_scale = project(tokens, updated, head_gain)
    new_weight = updated * row_scale[:, :1]
    return (new_weight, new_m, new_v, qkv)


def solution(mesh):
    return jax.shard_map(
        body,
        mesh=mesh,
        in_specs=(
            P("dp", "hidden"),
            P("dp", "hidden"),
            P("dp", "hidden"),
            P("dp", "hidden"),
            P("dp", "hidden"),
            P("hidden"),
        ),
        out_specs=(P("dp", "hidden"), P("dp", "hidden"), P("dp", "hidden"), P("dp", "hidden")),
        check_vma=False,
    )
```

```python
import math

import jax
import jax.numpy as jnp
from jax import lax
from jax.experimental import pallas as pl
from jax.experimental.pallas import tpu as pltpu
from jax.sharding import PartitionSpec as P

D = 8192
HD = 128
QR = 4096
KR = 512

NY, NZ, NX = 4, 8, 4
ROWS = 80
SPLIT = 32
KS = 2048
TOK = 512
COLS = 1280
HALF = KS // 2

beta_one = 0.9
beta_two = 0.95
learn_rate = 0.05
adam_eps = 1e-08
norm_eps = 1e-06
bias_one = 0.999973438601112
bias_two = 0.994079470779667

MESH = pl.DeviceIdType.MESH
FIRST, LAST, WHOLE, PAIR = 0, 1, 2, 3
SIGNS = (1, -1)


def side(s):
    return 0 if s > 0 else 1


def group_of(dz):
    if dz == 0:
        return 0
    if dz == 4:
        return 7
    return 2 * dz - 1 if dz > 0 else -2 * dz


def kernel(
    tok, weight, grad, adam_m, adam_v, gain, out, weight_out, m_out, v_out,
    state, wbuf, tokbuf, pbuf, inc, rel, fin, sq,
    s_ay, r_ay, s_az, r_az, s_bz, r_bz, s_by, r_by,
    s_x, r_inc, r_fin, r_sib, s_sq, r_sq, tok_sem, state_sem,
):
    dp = lax.axis_index("dp")
    x = lax.axis_index("hidden")
    y = lax.div(dp, 16)
    z = lax.rem(lax.div(dp, 2), NZ)
    c = lax.rem(dp, 2)

    def device(dy=0, dz=0, dx=0, core=None):
        yy = lax.rem(y + dy + NY, NY)
        zz = lax.rem(z + dz + NZ, NZ)
        return ((yy * NZ + zz) * 2 + (c if core is None else core), lax.rem(x + dx + NX, NX))

    def at_y(dy):
        return lax.rem(y + dy + NY, NY)

    def at_z(dz):
        return lax.rem(z + dz + NZ, NZ)

    def at_x(dx):
        return lax.rem(x + dx + NX, NX)

    y_dev = {s: device(dy=s) for s in SIGNS}
    z_dev = {s: device(dz=s) for s in SIGNS}
    x_dev = {(s, k): device(dx=s, core=k) for s in SIGNS for k in (0, 1)}
    x_two = device(dx=2)
    sibling = device(core=1 - c)

    barrier = pltpu.get_barrier_semaphore()
    partners = list(y_dev.values()) + list(z_dev.values()) + list(x_dev.values()) + [x_two, sibling]
    for partner in partners:
        pl.semaphore_signal(barrier, inc=1, device_id=partner, device_id_type=MESH)

    def copy(src, dst, send_sem, recv_sem, dev):
        return pltpu.make_async_remote_copy(
            src_ref=src, dst_ref=dst, send_sem=send_sem, recv_sem=recv_sem,
            device_id=dev, device_id_type=MESH,
        )

    loads = [
        pltpu.make_async_copy(src, state.at[i], state_sem.at[i])
        for i, src in enumerate((grad, adam_m, adam_v, weight))
    ]
    for load in loads:
        load.start()
    own_tok = pltpu.make_async_copy(tok, tokbuf.at[c], tok_sem.at[0])
    own_tok.start()
    for load in loads:
        load.wait()

    @pl.loop(0, ROWS // 16)
    def _(i):
        rows = pl.ds(pl.multiple_of(i * 16, 16), 16)
        g = state[0, rows]
        new_m = beta_one * state[1, rows] + (1.0 - beta_one) * g
        new_v = beta_two * state[2, rows] + (1.0 - beta_two) * g * g
        updated = state[3, rows] - learn_rate * (new_m / bias_one) / (jnp.sqrt(new_v / bias_two) + adam_eps)
        state[1, rows] = new_m
        state[2, rows] = new_v
        state[3, rows] = updated
        squares = updated * updated
        part = squares[:, 0:128]
        for k in range(1, KS // 128):
            part = part + squares[:, k * 128:(k + 1) * 128]
        sq[x, rows] = part

    pl.semaphore_wait(barrier, len(partners))

    sq_dev = {1: device(dx=1), 2: x_two, 3: device(dx=3)}
    sq_out = [copy(sq.at[x], sq.at[x], s_sq.at[d - 1], r_sq.at[d - 1], sq_dev[d]) for d in (1, 2, 3)]
    for d in (1, 0, 2):
        sq_out[d].start()
    tok_out = copy(tok, tokbuf.at[c], tok_sem.at[1], tok_sem.at[2], sibling)
    tok_out.start()
    for d in (1, 2, 3):
        slot = sq.at[at_x(-d)]
        copy(slot, slot, s_sq.at[d - 1], r_sq.at[d - 1], sibling).wait_recv()
    total = jnp.sum(sq[0] + sq[1] + sq[2] + sq[3], axis=1, keepdims=True)
    row_scale = 1.0 / jnp.sqrt(total / D + norm_eps)
    new_weight = state[3] * row_scale
    wbuf[z, y] = new_weight.astype(jnp.bfloat16)

    def part_a(zz, yy, s=None):
        ref = wbuf.at[zz, yy, pl.ds(0, SPLIT)]
        return ref if s is None else ref.at[:, pl.ds(side(s) * HALF, HALF)]

    def part_b(zz, yy, s=None):
        ref = wbuf.at[zz, yy, pl.ds(SPLIT, ROWS - SPLIT)]
        return ref if s is None else ref.at[:, pl.ds(side(s) * HALF, HALF)]

    y_order = (0, -1, 1, 2)

    def ay(hop, s):
        if hop == 1:
            ref = part_a(z, y)
        else:
            ref = part_a(z, at_y(-s), s)
        return copy(ref, ref, s_ay.at[hop - 1, side(s)], r_ay.at[hop - 1, side(s)], y_dev[s])

    def ay_recv(hop, s):
        ref = part_a(z, at_y(-s)) if hop == 1 else part_a(z, at_y(-2 * s), s)
        copy(ref, ref, s_ay.at[hop - 1, side(s)], r_ay.at[hop - 1, side(s)], y_dev[s]).wait_recv()

    def az(k, s, j):
        ref = part_a(at_z(-(k - 1) * s), at_y(y_order[j]), s if k == 4 else None)
        return copy(ref, ref, s_az.at[k - 1, side(s), j], r_az.at[k - 1, side(s), j], z_dev[s])

    def az_recv(k, s, j):
        ref = part_a(at_z(-k * s), at_y(y_order[j]), s if k == 4 else None)
        copy(ref, ref, s_az.at[k - 1, side(s), j], r_az.at[k - 1, side(s), j], z_dev[s]).wait_recv()

    def bz(k, s):
        ref = part_b(at_z(-(k - 1) * s), y, s if k == 4 else None)
        return copy(ref, ref, s_bz.at[k - 1, side(s)], r_bz.at[k - 1, side(s)], z_dev[s])

    def bz_recv(k, s):
        ref = part_b(at_z(-k * s), y, s if k == 4 else None)
        copy(ref, ref, s_bz.at[k - 1, side(s)], r_bz.at[k - 1, side(s)], z_dev[s]).wait_recv()

    def by(dz, hop, s):
        g = group_of(dz)
        ref = part_b(at_z(-dz), y) if hop == 1 else part_b(at_z(-dz), at_y(-s), s)
        return copy(ref, ref, s_by.at[g, hop - 1, side(s)], r_by.at[g, hop - 1, side(s)], y_dev[s])

    def by_recv(dz, hop, s):
        g = group_of(dz)
        ref = part_b(at_z(-dz), at_y(-s)) if hop == 1 else part_b(at_z(-dz), at_y(-2 * s), s)
        copy(ref, ref, s_by.at[g, hop - 1, side(s)], r_by.at[g, hop - 1, side(s)], y_dev[s]).wait_recv()

    for s in SIGNS:
        ay(1, s).start()
        bz(1, s).start()
    for s in SIGNS:
        by(0, 1, s).start()
        az(1, s, 0).start()

    def pass_z_first(k):
        for s in SIGNS:
            bz_recv(k, s)
            if k < 4:
                bz(k + 1, s).start()

    def start_y(dz):
        for s in SIGNS:
            by(dz, 1, s).start()

    def pass_y(dz):
        for s in SIGNS:
            by_recv(dz, 1, s)
            by(dz, 2, s).start()

    def pass_y_first(k, *js):
        for j in js:
            for s in SIGNS:
                az_recv(k, s, j)
                if k < 4:
                    az(k + 1, s, j).start()

    def arrive(dz):
        for s in SIGNS:
            by_recv(dz, 2, s)

    def open_a():
        for s in SIGNS:
            ay_recv(1, s)
            ay(2, s).start()
        pass_z_first(1)
        for j in (1, 2):
            for s in SIGNS:
                az(1, s, j).start()
        start_y(1)

    def close_a():
        for s in SIGNS:
            ay_recv(2, s)
        for s in SIGNS:
            az(1, s, 3).start()

    pieces = [
        (WHOLE, 0, [open_a, lambda: pass_y(0), lambda: start_y(-1), close_a], [lambda: pass_z_first(2), lambda: arrive(0)]),
        (PAIR, 1, [lambda: pass_y(1), lambda: start_y(2)], [lambda: pass_y_first(1, 0, 1, 2, 3)]),
        (LAST, 1, [lambda: pass_y(-1), lambda: start_y(-2)], [lambda: arrive(1)]),
        (LAST, 2, [lambda: pass_z_first(3), lambda: pass_y(2), lambda: start_y(3)], [lambda: arrive(-1)]),
        (LAST, 3, [lambda: pass_y(-2), lambda: start_y(-3), lambda: pass_y_first(2, 0, 1)], [lambda: arrive(2)]),
        (PAIR, 3, [], [lambda: pass_y_first(2, 2, 3)]),
        (LAST, 4, [lambda: pass_z_first(4), lambda: pass_y(3), lambda: start_y(4)], [lambda: arrive(-2)]),
        (LAST, 5, [lambda: pass_y(-3), lambda: pass_y_first(3, 0, 1)], [lambda: arrive(3)]),
        (PAIR, 5, [], [lambda: pass_y_first(3, 2, 3)]),
        (LAST, 6, [lambda: pass_y(4)], [lambda: arrive(-3)]),
        (WHOLE, 7, [lambda: pass_y_first(4, 0, 1, 2, 3)], [lambda: arrive(4)]),
    ]

    def look_up(p, column):
        value = jnp.int32(pieces[0][column])
        for i in range(1, len(pieces)):
            value = jnp.where(p == i, pieces[i][column], value)
        return value

    def in_turn(p, column):
        for i, piece in enumerate(pieces):
            if piece[column]:
                @pl.when(p == i)
                def _():
                    for act in piece[column]:
                        act()

    def by_kind(p, run):
        kind, g = look_up(p, 0), look_up(p, 1)
        pl.when(kind == WHOLE)(lambda: run([(g, WHOLE)]))
        pl.when(kind == PAIR)(lambda: run([(g, FIRST), (g + 1, FIRST)]))
        pl.when(kind == LAST)(lambda: run([(g, LAST)]))

    state[3] = new_weight
    stores = [
        pltpu.make_async_copy(state.at[i], dst, state_sem.at[i])
        for i, dst in ((1, m_out), (2, v_out), (3, weight_out))
    ]
    for store in stores:
        store.start()
    own_tok.wait()
    copy(tok, tokbuf.at[1 - c], tok_sem.at[1], tok_sem.at[2], sibling).wait_recv()

    def z_of(g):
        dz = jnp.where(lax.rem(g, 2) == 1, lax.div(g + 1, 2), -lax.div(g, 2))
        return lax.rem(z - dz + NZ, NZ)

    starts, lengths = {FIRST: 0, LAST: SPLIT, WHOLE: 0}, {FIRST: SPLIT, LAST: ROWS - SPLIT, WHOLE: ROWS}

    def rows_of(part):
        return pl.ds(starts[part], lengths[part])

    def place(zz, core, part):
        return pl.ds(pl.multiple_of(zz * (2 * ROWS) + core * ROWS + starts[part], 16), lengths[part])

    def send(g, part, i):
        zz = z_of(g)
        rows = rows_of(part)
        here = place(zz, c, part)
        k = part % 2
        src, dst, recv_sem, dev = (
            lambda: (pbuf.at[g, at_x(2), 0, rows], inc.at[g, 0, rows], r_inc.at[g, k, 0], device(dx=-1)),
            lambda: (pbuf.at[g, at_x(2), 1, rows], inc.at[g, 1, rows], r_inc.at[g, k, 1], device(dx=1)),
            lambda: (pbuf.at[g, at_x(-1), 1, rows], fin.at[0, here], r_fin.at[0, g, c, k], x_dev[-1, 1]),
            lambda: (pbuf.at[g, at_x(1), 0, rows], fin.at[1, here], r_fin.at[1, g, c, k], x_dev[1, 0]),
            lambda: (pbuf.at[g, x, 1 - c, rows], fin.at[2, here], r_sib.at[g, k], sibling),
            lambda: (rel.at[g, 0, rows], fin.at[0, here], r_fin.at[0, g, c, k], x_dev[-1, 0]),
            lambda: (rel.at[g, 1, rows], fin.at[1, here], r_fin.at[1, g, c, k], x_dev[1, 1]),
        )[i]()
        return copy(src, dst, s_x.at[g, k, i], recv_sem, dev)

    def multiply(blocks):
        taken = [wbuf[z_of(g), :, rows_of(part)].reshape(-1, KS) for g, part in blocks]
        product = lax.dot_general(
            taken[0] if len(taken) == 1 else jnp.concatenate(taken),
            tokbuf[...].reshape(2 * TOK, KS),
            (((1,), (1,)), ((), ())),
            preferred_element_type=jnp.float32,
        ).astype(jnp.bfloat16)
        for n, (g, part) in enumerate(blocks):
            size = NY * lengths[part]
            for half in (0, 1):
                block = product[n * size:(n + 1) * size, half * TOK:(half + 1) * TOK]
                pbuf[g, :, half, rows_of(part)] = block.reshape(NY, lengths[part], TOK)
        for i in range(5):
            for g, part in blocks:
                send(g, part, i).start()
        for g, part in blocks:
            fin[2, place(z_of(g), c, part)] = pbuf[g, x, c, rows_of(part)]

    def relay(blocks):
        for g, part in blocks:
            rows = rows_of(part)
            for i, owner in ((0, at_x(-1)), (1, at_x(1))):
                send(g, part, i).wait_recv()
                mixed = pbuf[g, owner, i, rows].astype(jnp.float32) + inc[g, i, rows].astype(jnp.float32)
                rel[g, i, rows] = mixed.astype(jnp.bfloat16)
                send(g, part, 5 + i).start()

    @pl.loop(0, len(pieces))
    def _(p):
        in_turn(p, 2)
        in_turn(p, 3)
        by_kind(p, multiply)

        @pl.when(p > 0)
        def _():
            by_kind(p - 1, relay)

    relay([(7, WHOLE)])

    def each_block(run):
        for g in (0, 7):
            run(g, WHOLE)

        @pl.loop(1, 7)
        def _(g):
            run(g, FIRST)
            run(g, LAST)

    def summed(g, part):
        for core in (0, 1):
            for i in (0, 1):
                slot = fin.at[i, place(z_of(g), core, part)]
                copy(slot, slot, s_x.at[0, 0, 0], r_fin.at[i, g, core, part % 2], sibling).wait_recv()
        slot = fin.at[2, place(z_of(g), 1 - c, part)]
        copy(slot, slot, s_x.at[0, 0, 0], r_sib.at[g, part % 2], sibling).wait_recv()

    each_block(summed)

    @pl.loop(0, COLS // HD)
    def _(h):
        rows = pl.ds(pl.multiple_of(h * HD, HD), HD)
        proj = (fin[0, rows].astype(jnp.float32) + fin[1, rows].astype(jnp.float32)) + fin[2, rows].astype(jnp.float32)
        mean_sq = jnp.sum(proj * proj, axis=0, keepdims=True) / HD
        is_qk = x * (COLS // HD) + h < (QR + KR) // HD
        factor = jnp.where(is_qk, 1.0 / jnp.sqrt(mean_sq + norm_eps), 1.0 / math.sqrt(D))
        out[:, rows] = ((proj * factor).T * gain[rows].reshape(1, HD)).astype(jnp.bfloat16)

    for store in stores:
        store.wait()
    for sq_send in sq_out:
        sq_send.wait_send()
    tok_out.wait_send()
    for s in SIGNS:
        for hop in (1, 2):
            ay(hop, s).wait_send()
        for k in range(1, 5):
            bz(k, s).wait_send()
            for j in range(4):
                az(k, s, j).wait_send()
        for dz in (0, 1, -1, 2, -2, 3, -3, 4):
            for hop in (1, 2):
                by(dz, hop, s).wait_send()

    def sent(g, part):
        for i in range(7):
            send(g, part, i).wait_send()

    each_block(sent)


def body(tokens, qkv_weight, grad, adam_m, adam_v, head_gain):
    dma = pltpu.SemaphoreType.DMA
    anywhere = pl.BlockSpec(memory_space=pl.ANY)
    state = jax.ShapeDtypeStruct((ROWS, KS), jnp.float32)
    vmem = pl.BlockSpec(memory_space=pltpu.VMEM)
    bf16 = jnp.bfloat16
    qkv, new_weight, new_m, new_v = pl.pallas_call(
        kernel,
        out_shape=(
            jax.ShapeDtypeStruct((TOK, COLS), bf16),
            state, state, state,
        ),
        in_specs=[pl.BlockSpec(memory_space=pltpu.HBM)] * 5 + [vmem],
        out_specs=(vmem, anywhere, anywhere, anywhere),
        scratch_shapes=[
            pltpu.VMEM((4, ROWS, KS), jnp.float32),
            pltpu.VMEM((NZ, NY, ROWS, KS), bf16),
            pltpu.VMEM((2, TOK, KS), bf16),
            pltpu.VMEM((8, NX, 2, ROWS, TOK), bf16),
            pltpu.VMEM((8, 2, ROWS, TOK), bf16),
            pltpu.VMEM((8, 2, ROWS, TOK), bf16),
            pltpu.VMEM((3, COLS, TOK), bf16),
            pltpu.VMEM((NX, ROWS, 128), jnp.float32),
            dma((2, 2)), dma((2, 2)),
            dma((4, 2, 4)), dma((4, 2, 4)),
            dma((4, 2)), dma((4, 2)),
            dma((8, 2, 2)), dma((8, 2, 2)),
            dma((8, 2, 7)), dma((8, 2, 2)), dma((2, 8, 2, 2)), dma((8, 2)),
            dma((3,)), dma((3,)), dma((3,)), dma((4,)),
        ],
        compiler_params=pltpu.CompilerParams(
            collective_id=0, has_side_effects=True, vmem_limit_bytes=60 * 2**20
        ),
        cost_estimate=pl.CostEstimate(
            flops=2 * 2 * TOK * KS * NZ * NY * ROWS, bytes_accessed=4 * 2**20, transcendentals=0
        ),
    )(tokens, qkv_weight, grad, adam_m, adam_v, head_gain)
    return (new_weight, new_m, new_v, qkv)


def solution(mesh):
    return jax.shard_map(
        body,
        mesh=mesh,
        in_specs=(
            P("dp", "hidden"),
            P("dp", "hidden"),
            P("dp", "hidden"),
            P("dp", "hidden"),
            P("dp", "hidden"),
            P("hidden"),
        ),
        out_specs=(P("dp", "hidden"), P("dp", "hidden"), P("dp", "hidden"), P("dp", "hidden")),
        check_vma=False,
    )
```

```python
import math

import jax
import jax.numpy as jnp
from jax import lax
from jax.experimental import pallas as pl
from jax.experimental.pallas import tpu as pltpu
from jax.sharding import PartitionSpec as P

D = 8192
HD = 128
QR = 4096
KR = 512

NY, NZ, NX = 4, 8, 4
ROWS = 80
SPLIT = 32
KS = 2048
TOK = 512
COLS = 1280
HALF = KS // 2

beta_one = 0.9
beta_two = 0.95
learn_rate = 0.05
adam_eps = 1e-08
norm_eps = 1e-06
bias_one = 0.999973438601112
bias_two = 0.994079470779667

MESH = pl.DeviceIdType.MESH
FIRST, LAST, WHOLE, PAIR = 0, 1, 2, 3
SIGNS = (1, -1)


def side(s):
    return 0 if s > 0 else 1


def group_of(dz):
    if dz == 0:
        return 0
    if dz == 4:
        return 7
    return 2 * dz - 1 if dz > 0 else -2 * dz


def kernel(
    tok, weight, grad, adam_m, adam_v, head_gain, out, weight_out, m_out, v_out,
    state, wbuf, tokbuf, pbuf, inc, rel, fin, sq, pad, near, scales, columns, gain,
    s_ay, r_ay, s_az, r_az, s_bz, r_bz, s_by, r_by,
    s_x, r_inc, r_fin, r_sib, s_sq, r_sq, s_near, r_near, s_far, r_far, swap_sem, gain_sem, tok_sem, state_sem,
):
    dp = lax.axis_index("dp")
    x = lax.axis_index("hidden")
    y = lax.div(dp, 16)
    z = lax.rem(lax.div(dp, 2), NZ)
    c = lax.rem(dp, 2)

    def device(dy=0, dz=0, dx=0, core=None):
        yy = lax.rem(y + dy + NY, NY)
        zz = lax.rem(z + dz + NZ, NZ)
        return ((yy * NZ + zz) * 2 + (c if core is None else core), lax.rem(x + dx + NX, NX))

    def at_y(dy):
        return lax.rem(y + dy + NY, NY)

    def at_z(dz):
        return lax.rem(z + dz + NZ, NZ)

    def at_x(dx):
        return lax.rem(x + dx + NX, NX)

    y_dev = {s: device(dy=s) for s in SIGNS}
    z_dev = {s: device(dz=s) for s in SIGNS}
    x_dev = {(s, k): device(dx=s, core=k) for s in SIGNS for k in (0, 1)}
    x_two = device(dx=2)
    sibling = device(core=1 - c)

    barrier = pltpu.get_barrier_semaphore()
    partners = list(y_dev.values()) + list(z_dev.values()) + list(x_dev.values()) + [x_two, sibling]
    y_two = device(dy=2)
    z_far = {d: device(dz=d) for d in range(2, NZ - 1)}
    partners += [y_two] + list(z_far.values())
    for partner in partners:
        pl.semaphore_signal(barrier, inc=1, device_id=partner, device_id_type=MESH)

    def copy(src, dst, send_sem, recv_sem, dev):
        return pltpu.make_async_remote_copy(
            src_ref=src, dst_ref=dst, send_sem=send_sem, recv_sem=recv_sem,
            device_id=dev, device_id_type=MESH,
        )

    loads = [
        pltpu.make_async_copy(src, state.at[i], state_sem.at[i])
        for i, src in enumerate((grad, adam_m, adam_v, weight))
    ]
    for load in loads:
        load.start()
    own_tok = pltpu.make_async_copy(tok, tokbuf.at[c], tok_sem.at[0])
    own_tok.start()
    gain_load = pltpu.make_async_copy(head_gain, gain, gain_sem.at[0])
    gain_load.start()
    for load in loads:
        load.wait()

    @pl.loop(0, ROWS // 16)
    def _(i):
        rows = pl.ds(pl.multiple_of(i * 16, 16), 16)
        g = state[0, rows]
        new_m = beta_one * state[1, rows] + (1.0 - beta_one) * g
        new_v = beta_two * state[2, rows] + (1.0 - beta_two) * g * g
        updated = state[3, rows] - learn_rate * (new_m / bias_one) / (jnp.sqrt(new_v / bias_two) + adam_eps)
        state[1, rows] = new_m
        state[2, rows] = new_v
        state[3, rows] = updated
        wbuf[z, y, rows] = updated.astype(jnp.bfloat16)
        squares = updated * updated
        part = squares[:, 0:128]
        for k in range(1, KS // 128):
            part = part + squares[:, k * 128:(k + 1) * 128]
        sq[x, rows] = part

    pl.semaphore_wait(barrier, len(partners))

    def part_a(zz, yy, s=None):
        ref = wbuf.at[zz, yy, pl.ds(0, SPLIT)]
        return ref if s is None else ref.at[:, pl.ds(side(s) * HALF, HALF)]

    def part_b(zz, yy, s=None):
        ref = wbuf.at[zz, yy, pl.ds(SPLIT, ROWS - SPLIT)]
        return ref if s is None else ref.at[:, pl.ds(side(s) * HALF, HALF)]

    y_order = (0, -1, 1, 2)

    def ay(hop, s):
        if hop == 1:
            ref = part_a(z, y)
        else:
            ref = part_a(z, at_y(-s), s)
        return copy(ref, ref, s_ay.at[hop - 1, side(s)], r_ay.at[hop - 1, side(s)], y_dev[s])

    def ay_recv(hop, s):
        ref = part_a(z, at_y(-s)) if hop == 1 else part_a(z, at_y(-2 * s), s)
        copy(ref, ref, s_ay.at[hop - 1, side(s)], r_ay.at[hop - 1, side(s)], y_dev[s]).wait_recv()

    def az(k, s, j):
        ref = part_a(at_z(-(k - 1) * s), at_y(y_order[j]), s if k == 4 else None)
        return copy(ref, ref, s_az.at[k - 1, side(s), j], r_az.at[k - 1, side(s), j], z_dev[s])

    def az_recv(k, s, j):
        ref = part_a(at_z(-k * s), at_y(y_order[j]), s if k == 4 else None)
        copy(ref, ref, s_az.at[k - 1, side(s), j], r_az.at[k - 1, side(s), j], z_dev[s]).wait_recv()

    def bz(k, s):
        ref = part_b(at_z(-(k - 1) * s), y, s if k == 4 else None)
        return copy(ref, ref, s_bz.at[k - 1, side(s)], r_bz.at[k - 1, side(s)], z_dev[s])

    def bz_recv(k, s):
        ref = part_b(at_z(-k * s), y, s if k == 4 else None)
        copy(ref, ref, s_bz.at[k - 1, side(s)], r_bz.at[k - 1, side(s)], z_dev[s]).wait_recv()

    def by(dz, hop, s):
        g = group_of(dz)
        ref = part_b(at_z(-dz), y) if hop == 1 else part_b(at_z(-dz), at_y(-s), s)
        return copy(ref, ref, s_by.at[g, hop - 1, side(s)], r_by.at[g, hop - 1, side(s)], y_dev[s])

    def by_recv(dz, hop, s):
        g = group_of(dz)
        ref = part_b(at_z(-dz), at_y(-s)) if hop == 1 else part_b(at_z(-dz), at_y(-2 * s), s)
        copy(ref, ref, s_by.at[g, hop - 1, side(s)], r_by.at[g, hop - 1, side(s)], y_dev[s]).wait_recv()

    for s in SIGNS:
        ay(1, s).start()
        bz(1, s).start()
    for s in SIGNS:
        by(0, 1, s).start()
        az(1, s, 0).start()

    sq_dev = {1: device(dx=1), 2: x_two, 3: device(dx=3)}

    def sq_copy(d, slot):
        return copy(sq.at[slot], sq.at[slot], s_sq.at[d - 1], r_sq.at[d - 1], sq_dev[d])

    for d in (2, 1, 3):
        sq_copy(d, x).start()
    tok_out = copy(tok, tokbuf.at[c], tok_sem.at[1], tok_sem.at[2], sibling)
    tok_out.start()

    def stores():
        return [
            pltpu.make_async_copy(state.at[i], dst, state_sem.at[i])
            for i, dst in ((1, m_out), (2, v_out), (3, weight_out))
        ]

    def scale_rows():
        for d in (1, 2, 3):
            sq_copy(d, at_x(-d)).wait_recv()
        total = jnp.sum(sq[0] + sq[1] + sq[2] + sq[3], axis=1, keepdims=True)
        row_scale = 1.0 / jnp.sqrt(total / D + norm_eps)
        pad[...] = jnp.ones_like(pad)
        pad[0:ROWS] = jnp.broadcast_to(row_scale, (ROWS, 128))
        near[y] = pad[...].T[0:8]
        for d in (1, 2, 3):
            near_copy(d, y).start()
        state[3] = state[3] * row_scale
        for store in stores():
            store.start()

    def near_copy(d, slot):
        dev = y_two if d == 2 else y_dev[1 if d == 1 else -1]
        return copy(near.at[slot], near.at[slot], s_near.at[d - 1], r_near.at[d - 1], dev)

    def far_copy(d):
        dev = z_far[d] if d in z_far else z_dev[1 if d == 1 else -1]
        return copy(near.at[x], scales.at[c, z], s_far.at[d - 1], r_far.at[d - 1], dev)

    def far_recv(d):
        slot = scales.at[c, at_z(-d)]
        copy(slot, slot, s_far.at[d - 1], r_far.at[d - 1], sibling).wait_recv()

    def swap(core):
        return copy(scales.at[core], scales.at[core], swap_sem.at[0], swap_sem.at[1], sibling)

    def pass_scales():
        for d in (1, 2, 3):
            near_copy(d, at_y(-d)).wait_recv()
        scales[c, z] = near[x]
        for d in range(1, NZ):
            far_copy(d).start()

    def swap_scales():
        for d in range(1, NZ):
            far_recv(d)
        swap(c).start()

    def take_scales():
        swap(1 - c).wait_recv()

        @pl.loop(0, NZ)
        def _(zz):
            for core in (0, 1):
                turned = jnp.broadcast_to(scales[core, zz, 0:1], (128, 128)).T
                columns[pl.ds(pl.multiple_of(zz * (2 * ROWS) + core * ROWS, 16), ROWS)] = turned[0:ROWS]

    def pass_z_first(k):
        for s in SIGNS:
            bz_recv(k, s)
            if k < 4:
                bz(k + 1, s).start()

    def start_y(dz):
        for s in SIGNS:
            by(dz, 1, s).start()

    def pass_y(dz):
        for s in SIGNS:
            by_recv(dz, 1, s)
            by(dz, 2, s).start()

    def pass_y_first(k, *js):
        for j in js:
            for s in SIGNS:
                az_recv(k, s, j)
                if k < 4:
                    az(k + 1, s, j).start()

    def arrive(dz):
        for s in SIGNS:
            by_recv(dz, 2, s)

    def take_tokens():
        own_tok.wait()
        gain_load.wait()
        copy(tok, tokbuf.at[1 - c], tok_sem.at[1], tok_sem.at[2], sibling).wait_recv()

    def open_a():
        for s in SIGNS:
            ay_recv(1, s)
            ay(2, s).start()
        pass_z_first(1)
        for j in (1, 2):
            for s in SIGNS:
                az(1, s, j).start()
        start_y(1)

    def close_a():
        for s in SIGNS:
            ay_recv(2, s)
        for s in SIGNS:
            az(1, s, 3).start()

    pieces = [
        (WHOLE, 0, [open_a, scale_rows, lambda: pass_y(0), lambda: start_y(-1), close_a], [lambda: pass_z_first(2), take_tokens, lambda: arrive(0)]),
        (PAIR, 1, [lambda: pass_y(1), lambda: start_y(2)], [lambda: pass_y_first(1, 0, 1, 2, 3)]),
        (LAST, 1, [lambda: pass_y(-1), lambda: start_y(-2)], [lambda: arrive(1)]),
        (LAST, 2, [lambda: pass_z_first(3), lambda: pass_y(2), lambda: start_y(3), pass_scales], [lambda: arrive(-1)]),
        (LAST, 3, [lambda: pass_y(-2), lambda: start_y(-3), lambda: pass_y_first(2, 0, 1)], [lambda: arrive(2)]),
        (PAIR, 3, [], [lambda: pass_y_first(2, 2, 3)]),
        (LAST, 4, [lambda: pass_z_first(4), lambda: pass_y(3), lambda: start_y(4), swap_scales], [lambda: arrive(-2)]),
        (LAST, 5, [lambda: pass_y(-3), lambda: pass_y_first(3, 0, 1)], [lambda: arrive(3)]),
        (PAIR, 5, [take_scales], [lambda: pass_y_first(3, 2, 3)]),
        (LAST, 6, [lambda: pass_y(4)], [lambda: arrive(-3)]),
        (WHOLE, 7, [lambda: pass_y_first(4, 0, 1, 2, 3)], [lambda: arrive(4)]),
    ]

    def look_up(p, column):
        value = jnp.int32(pieces[0][column])
        for i in range(1, len(pieces)):
            value = jnp.where(p == i, pieces[i][column], value)
        return value

    def in_turn(p, column):
        for i, piece in enumerate(pieces):
            if piece[column]:
                @pl.when(p == i)
                def _():
                    for act in piece[column]:
                        act()

    def by_kind(p, run):
        kind, g = look_up(p, 0), look_up(p, 1)
        pl.when(kind == WHOLE)(lambda: run([(g, WHOLE)]))
        pl.when(kind == PAIR)(lambda: run([(g, FIRST), (g + 1, FIRST)]))
        pl.when(kind == LAST)(lambda: run([(g, LAST)]))

    def z_of(g):
        dz = jnp.where(lax.rem(g, 2) == 1, lax.div(g + 1, 2), -lax.div(g, 2))
        return lax.rem(z - dz + NZ, NZ)

    starts, lengths = {FIRST: 0, LAST: SPLIT, WHOLE: 0}, {FIRST: SPLIT, LAST: ROWS - SPLIT, WHOLE: ROWS}

    def rows_of(part):
        return pl.ds(starts[part], lengths[part])

    def place(zz, core, part):
        return pl.ds(pl.multiple_of(zz * (2 * ROWS) + core * ROWS + starts[part], 16), lengths[part])

    def send(g, part, i):
        zz = z_of(g)
        rows = rows_of(part)
        here = place(zz, c, part)
        k = part % 2
        src, dst, recv_sem, dev = (
            lambda: (pbuf.at[g, at_x(2), 0, rows], inc.at[g, 0, rows], r_inc.at[g, k, 0], device(dx=-1)),
            lambda: (pbuf.at[g, at_x(2), 1, rows], inc.at[g, 1, rows], r_inc.at[g, k, 1], device(dx=1)),
            lambda: (pbuf.at[g, at_x(-1), 1, rows], fin.at[0, here], r_fin.at[0, g, c, k], x_dev[-1, 1]),
            lambda: (pbuf.at[g, at_x(1), 0, rows], fin.at[1, here], r_fin.at[1, g, c, k], x_dev[1, 0]),
            lambda: (pbuf.at[g, x, 1 - c, rows], fin.at[2, here], r_sib.at[g, k], sibling),
            lambda: (rel.at[g, 0, rows], fin.at[0, here], r_fin.at[0, g, c, k], x_dev[-1, 0]),
            lambda: (rel.at[g, 1, rows], fin.at[1, here], r_fin.at[1, g, c, k], x_dev[1, 1]),
        )[i]()
        return copy(src, dst, s_x.at[g, k, i], recv_sem, dev)

    def multiply(blocks):
        taken = [wbuf[z_of(g), :, rows_of(part)].reshape(-1, KS) for g, part in blocks]
        product = lax.dot_general(
            taken[0] if len(taken) == 1 else jnp.concatenate(taken),
            tokbuf[...].reshape(2 * TOK, KS),
            (((1,), (1,)), ((), ())),
            preferred_element_type=jnp.float32,
        ).astype(jnp.bfloat16)
        for n, (g, part) in enumerate(blocks):
            size = NY * lengths[part]
            for half in (0, 1):
                block = product[n * size:(n + 1) * size, half * TOK:(half + 1) * TOK]
                pbuf[g, :, half, rows_of(part)] = block.reshape(NY, lengths[part], TOK)
        for i in range(5):
            for g, part in blocks:
                send(g, part, i).start()
        for g, part in blocks:
            fin[2, place(z_of(g), c, part)] = pbuf[g, x, c, rows_of(part)]

    def relay(blocks):
        for g, part in blocks:
            rows = rows_of(part)
            for i, owner in ((0, at_x(-1)), (1, at_x(1))):
                send(g, part, i).wait_recv()
                mixed = pbuf[g, owner, i, rows].astype(jnp.float32) + inc[g, i, rows].astype(jnp.float32)
                rel[g, i, rows] = mixed.astype(jnp.bfloat16)
                send(g, part, 5 + i).start()

    @pl.loop(0, len(pieces))
    def _(p):
        in_turn(p, 2)
        in_turn(p, 3)
        by_kind(p, multiply)

        @pl.when(p > 0)
        def _():
            by_kind(p - 1, relay)

    def each_block(first, last, run):
        @pl.loop(max(first, 1), min(last, 7))
        def _(g):
            run(g, FIRST)
            run(g, LAST)

        for g in (0, 7):
            if first <= g < last:
                run(g, WHOLE)

    def summed(g, part):
        for core in (0, 1):
            for i in (0, 1):
                slot = fin.at[i, place(z_of(g), core, part)]
                copy(slot, slot, s_x.at[0, 0, 0], r_fin.at[i, g, core, part % 2], sibling).wait_recv()
        slot = fin.at[2, place(z_of(g), 1 - c, part)]
        copy(slot, slot, s_x.at[0, 0, 0], r_sib.at[g, part % 2], sibling).wait_recv()

    heads = COLS // HD
    behind = lax.div(at_z(5) * (2 * ROWS) + HD - 1, HD)

    def finish(i):
        h = lax.rem(behind + i, heads)
        rows = pl.ds(pl.multiple_of(h * HD, HD), HD)
        proj = (fin[0, rows].astype(jnp.float32) + fin[1, rows].astype(jnp.float32)) + fin[2, rows].astype(jnp.float32)
        proj = proj * columns[rows, 0:1]
        mean_sq = jnp.sum(proj * proj, axis=0, keepdims=True) / HD
        is_qk = x * heads + h < (QR + KR) // HD
        factor = jnp.where(is_qk, 1.0 / jnp.sqrt(mean_sq + norm_eps), 1.0 / math.sqrt(D))
        out[:, rows] = ((proj * factor).T * gain[rows].reshape(1, HD)).astype(jnp.bfloat16)

    each_block(0, 6, summed)
    pl.loop(0, 6)(finish)
    relay([(7, WHOLE)])
    each_block(6, 8, summed)
    pl.loop(6, heads)(finish)

    for store in stores():
        store.wait()
    for d in (1, 2, 3):
        sq_copy(d, x).wait_send()
        near_copy(d, y).wait_send()
    for d in range(1, NZ):
        far_copy(d).wait_send()
    swap(c).wait_send()
    tok_out.wait_send()
    for s in SIGNS:
        for hop in (1, 2):
            ay(hop, s).wait_send()
        for k in range(1, 5):
            bz(k, s).wait_send()
            for j in range(4):
                az(k, s, j).wait_send()
        for dz in (0, 1, -1, 2, -2, 3, -3, 4):
            for hop in (1, 2):
                by(dz, hop, s).wait_send()

    def sent(g, part):
        for i in range(7):
            send(g, part, i).wait_send()

    each_block(0, 8, sent)


def body(tokens, qkv_weight, grad, adam_m, adam_v, head_gain):
    dma = pltpu.SemaphoreType.DMA
    anywhere = pl.BlockSpec(memory_space=pl.ANY)
    state = jax.ShapeDtypeStruct((ROWS, KS), jnp.float32)
    vmem = pl.BlockSpec(memory_space=pltpu.VMEM)
    bf16 = jnp.bfloat16
    qkv, new_weight, new_m, new_v = pl.pallas_call(
        kernel,
        out_shape=(
            jax.ShapeDtypeStruct((TOK, COLS), bf16),
            state, state, state,
        ),
        in_specs=[pl.BlockSpec(memory_space=pltpu.HBM)] * 6,
        out_specs=(vmem, anywhere, anywhere, anywhere),
        scratch_shapes=[
            pltpu.VMEM((4, ROWS, KS), jnp.float32),
            pltpu.VMEM((NZ, NY, ROWS, KS), bf16),
            pltpu.VMEM((2, TOK, KS), bf16),
            pltpu.VMEM((8, NX, 2, ROWS, TOK), bf16),
            pltpu.VMEM((8, 2, ROWS, TOK), bf16),
            pltpu.VMEM((8, 2, ROWS, TOK), bf16),
            pltpu.VMEM((3, COLS, TOK), bf16),
            pltpu.VMEM((NX, ROWS, 128), jnp.float32),
            pltpu.VMEM((128, 128), jnp.float32),
            pltpu.VMEM((NY, 8, 128), jnp.float32),
            pltpu.VMEM((2, NZ, 8, 128), jnp.float32),
            pltpu.VMEM((COLS, 128), jnp.float32),
            pltpu.VMEM((COLS,), jnp.float32),
            dma((2, 2)), dma((2, 2)),
            dma((4, 2, 4)), dma((4, 2, 4)),
            dma((4, 2)), dma((4, 2)),
            dma((8, 2, 2)), dma((8, 2, 2)),
            dma((8, 2, 7)), dma((8, 2, 2)), dma((2, 8, 2, 2)), dma((8, 2)),
            dma((3,)), dma((3,)), dma((3,)), dma((3,)), dma((7,)), dma((7,)), dma((2,)), dma((1,)), dma((3,)), dma((4,)),
        ],
        compiler_params=pltpu.CompilerParams(
            collective_id=0, has_side_effects=True, vmem_limit_bytes=52 * 2**20
        ),
        cost_estimate=pl.CostEstimate(
            flops=2 * 2 * TOK * KS * NZ * NY * ROWS, bytes_accessed=4 * 2**20, transcendentals=0
        ),
    )(tokens, qkv_weight, grad, adam_m, adam_v, head_gain)
    return (new_weight, new_m, new_v, qkv)


def solution(mesh):
    return jax.shard_map(
        body,
        mesh=mesh,
        in_specs=(
            P("dp", "hidden"),
            P("dp", "hidden"),
            P("dp", "hidden"),
            P("dp", "hidden"),
            P("dp", "hidden"),
            P("hidden"),
        ),
        out_specs=(P("dp", "hidden"), P("dp", "hidden"), P("dp", "hidden"), P("dp", "hidden")),
        check_vma=False,
    )
```

```python
import math

import jax
import jax.numpy as jnp
from jax import lax
from jax.experimental import pallas as pl
from jax.experimental.pallas import tpu as pltpu
from jax.sharding import PartitionSpec as P

D = 8192
HD = 128
QR = 4096
KR = 512

NY, NZ, NX = 4, 8, 4
ROWS = 80
SPLIT = 32
KS = 2048
TOK = 512
COLS = 1280
HALF = KS // 2

beta_one = 0.9
beta_two = 0.95
learn_rate = 0.05
adam_eps = 1e-08
norm_eps = 1e-06
bias_one = 0.999973438601112
bias_two = 0.994079470779667

MESH = pl.DeviceIdType.MESH
FIRST, LAST, WHOLE, PAIR = 0, 1, 2, 3
SIGNS = (1, -1)


def side(s):
    return 0 if s > 0 else 1


def group_of(dz):
    if dz == 0:
        return 0
    if dz == 4:
        return 7
    return 2 * dz - 1 if dz > 0 else -2 * dz


def kernel(
    tok, weight, grad, adam_m, adam_v, head_gain, out, weight_out, m_out, v_out,
    state, wbuf, tokbuf, pbuf, inc, rel, fin, sq, pad, near, scales, columns, gain,
    s_ay, r_ay, s_az, r_az, s_bz, r_bz, s_by, r_by,
    s_x, r_inc, r_fin, r_sib, s_sq, r_sq, s_near, r_near, s_far, r_far, swap_sem, gain_sem, tok_sem, load_sem, state_sem,
):
    dp = lax.axis_index("dp")
    x = lax.axis_index("hidden")
    y = lax.div(dp, 16)
    z = lax.rem(lax.div(dp, 2), NZ)
    c = lax.rem(dp, 2)

    def device(dy=0, dz=0, dx=0, core=None):
        yy = lax.rem(y + dy + NY, NY)
        zz = lax.rem(z + dz + NZ, NZ)
        return ((yy * NZ + zz) * 2 + (c if core is None else core), lax.rem(x + dx + NX, NX))

    def at_y(dy):
        return lax.rem(y + dy + NY, NY)

    def at_z(dz):
        return lax.rem(z + dz + NZ, NZ)

    def at_x(dx):
        return lax.rem(x + dx + NX, NX)

    y_dev = {s: device(dy=s) for s in SIGNS}
    z_dev = {s: device(dz=s) for s in SIGNS}
    x_dev = {(s, k): device(dx=s, core=k) for s in SIGNS for k in (0, 1)}
    x_two = device(dx=2)
    sibling = device(core=1 - c)

    barrier = pltpu.get_barrier_semaphore()
    partners = list(y_dev.values()) + list(z_dev.values()) + list(x_dev.values()) + [x_two, sibling]
    y_two = device(dy=2)
    z_far = {d: device(dz=d) for d in range(2, NZ - 1)}
    partners += [y_two] + list(z_far.values())
    for partner in partners:
        pl.semaphore_signal(barrier, inc=1, device_id=partner, device_id_type=MESH)

    def copy(src, dst, send_sem, recv_sem, dev):
        return pltpu.make_async_remote_copy(
            src_ref=src, dst_ref=dst, send_sem=send_sem, recv_sem=recv_sem,
            device_id=dev, device_id_type=MESH,
        )

    def load(i, n):
        rows = pl.ds(pl.multiple_of(i * 16, 16), 16)
        src = (grad, adam_m, adam_v, weight)[n]
        return pltpu.make_async_copy(src.at[rows], state.at[n, rows], load_sem.at[i, n])

    for i in range(ROWS // 16):
        for n in range(4):
            load(i, n).start()
    own_tok = pltpu.make_async_copy(tok, tokbuf.at[c], tok_sem.at[0])
    own_tok.start()
    gain_load = pltpu.make_async_copy(head_gain, gain, gain_sem.at[0])
    gain_load.start()

    def adam(i):
        for n in range(4):
            load(i, n).wait()
        rows = pl.ds(pl.multiple_of(i * 16, 16), 16)
        g = state[0, rows]
        new_m = beta_one * state[1, rows] + (1.0 - beta_one) * g
        new_v = beta_two * state[2, rows] + (1.0 - beta_two) * g * g
        step = (learn_rate / bias_one) * new_m / (jnp.sqrt((1.0 / bias_two) * new_v) + adam_eps)
        updated = state[3, rows] - step
        state[1, rows] = new_m
        state[2, rows] = new_v
        state[3, rows] = updated
        wbuf[z, y, rows] = updated.astype(jnp.bfloat16)
        squares = updated * updated
        part = squares[:, 0:128]
        for k in range(1, KS // 128):
            part = part + squares[:, k * 128:(k + 1) * 128]
        sq[x, rows] = part

    pl.loop(0, SPLIT // 16)(adam)
    pl.semaphore_wait(barrier, len(partners))

    def part_a(zz, yy, s=None):
        ref = wbuf.at[zz, yy, pl.ds(0, SPLIT)]
        return ref if s is None else ref.at[:, pl.ds(side(s) * HALF, HALF)]

    def part_b(zz, yy, s=None):
        ref = wbuf.at[zz, yy, pl.ds(SPLIT, ROWS - SPLIT)]
        return ref if s is None else ref.at[:, pl.ds(side(s) * HALF, HALF)]

    y_order = (0, -1, 1, 2)

    def ay(hop, s):
        if hop == 1:
            ref = part_a(z, y)
        else:
            ref = part_a(z, at_y(-s), s)
        return copy(ref, ref, s_ay.at[hop - 1, side(s)], r_ay.at[hop - 1, side(s)], y_dev[s])

    def ay_recv(hop, s):
        ref = part_a(z, at_y(-s)) if hop == 1 else part_a(z, at_y(-2 * s), s)
        copy(ref, ref, s_ay.at[hop - 1, side(s)], r_ay.at[hop - 1, side(s)], y_dev[s]).wait_recv()

    def az(k, s, j):
        ref = part_a(at_z(-(k - 1) * s), at_y(y_order[j]), s if k == 4 else None)
        return copy(ref, ref, s_az.at[k - 1, side(s), j], r_az.at[k - 1, side(s), j], z_dev[s])

    def az_recv(k, s, j):
        ref = part_a(at_z(-k * s), at_y(y_order[j]), s if k == 4 else None)
        copy(ref, ref, s_az.at[k - 1, side(s), j], r_az.at[k - 1, side(s), j], z_dev[s]).wait_recv()

    def bz(k, s):
        ref = part_b(at_z(-(k - 1) * s), y, s if k == 4 else None)
        return copy(ref, ref, s_bz.at[k - 1, side(s)], r_bz.at[k - 1, side(s)], z_dev[s])

    def bz_recv(k, s):
        ref = part_b(at_z(-k * s), y, s if k == 4 else None)
        copy(ref, ref, s_bz.at[k - 1, side(s)], r_bz.at[k - 1, side(s)], z_dev[s]).wait_recv()

    def by(dz, hop, s):
        g = group_of(dz)
        ref = part_b(at_z(-dz), y) if hop == 1 else part_b(at_z(-dz), at_y(-s), s)
        return copy(ref, ref, s_by.at[g, hop - 1, side(s)], r_by.at[g, hop - 1, side(s)], y_dev[s])

    def by_recv(dz, hop, s):
        g = group_of(dz)
        ref = part_b(at_z(-dz), at_y(-s)) if hop == 1 else part_b(at_z(-dz), at_y(-2 * s), s)
        copy(ref, ref, s_by.at[g, hop - 1, side(s)], r_by.at[g, hop - 1, side(s)], y_dev[s]).wait_recv()

    for s in SIGNS:
        ay(1, s).start()
    pl.loop(SPLIT // 16, ROWS // 16)(adam)
    for s in SIGNS:
        bz(1, s).start()
        by(0, 1, s).start()
    for s in SIGNS:
        az(1, s, 0).start()

    sq_dev = {1: device(dx=1), 2: x_two, 3: device(dx=3)}

    def sq_copy(d, slot):
        return copy(sq.at[slot], sq.at[slot], s_sq.at[d - 1], r_sq.at[d - 1], sq_dev[d])

    for d in (2, 1, 3):
        sq_copy(d, x).start()
    tok_out = copy(tok, tokbuf.at[c], tok_sem.at[1], tok_sem.at[2], sibling)
    tok_out.start()

    def stores():
        return [
            pltpu.make_async_copy(state.at[i], dst, state_sem.at[i])
            for i, dst in ((1, m_out), (2, v_out), (3, weight_out))
        ]

    def scale_rows():
        for d in (1, 2, 3):
            sq_copy(d, at_x(-d)).wait_recv()
        total = jnp.sum(sq[0] + sq[1] + sq[2] + sq[3], axis=1, keepdims=True)
        row_scale = 1.0 / jnp.sqrt(total / D + norm_eps)
        pad[...] = jnp.ones_like(pad)
        pad[0:ROWS] = jnp.broadcast_to(row_scale, (ROWS, 128))
        near[y] = pad[...].T[0:8]
        for d in (1, 2, 3):
            near_copy(d, y).start()
        state[3] = state[3] * row_scale
        for store in stores():
            store.start()

    def near_copy(d, slot):
        dev = y_two if d == 2 else y_dev[1 if d == 1 else -1]
        return copy(near.at[slot], near.at[slot], s_near.at[d - 1], r_near.at[d - 1], dev)

    def far_copy(d):
        dev = z_far[d] if d in z_far else z_dev[1 if d == 1 else -1]
        return copy(near.at[x], scales.at[c, z], s_far.at[d - 1], r_far.at[d - 1], dev)

    def far_recv(d):
        slot = scales.at[c, at_z(-d)]
        copy(slot, slot, s_far.at[d - 1], r_far.at[d - 1], sibling).wait_recv()

    def swap(core):
        return copy(scales.at[core], scales.at[core], swap_sem.at[0], swap_sem.at[1], sibling)

    def pass_scales():
        for d in (1, 2, 3):
            near_copy(d, at_y(-d)).wait_recv()
        scales[c, z] = near[x]
        for d in range(1, NZ):
            far_copy(d).start()

    def swap_scales():
        for d in range(1, NZ):
            far_recv(d)
        swap(c).start()

    def take_scales():
        swap(1 - c).wait_recv()

        @pl.loop(0, NZ)
        def _(zz):
            for core in (0, 1):
                turned = jnp.broadcast_to(scales[core, zz, 0:1], (128, 128)).T
                columns[pl.ds(pl.multiple_of(zz * (2 * ROWS) + core * ROWS, 16), ROWS)] = turned[0:ROWS]

    def pass_z_first(k):
        for s in SIGNS:
            bz_recv(k, s)
            if k < 4:
                bz(k + 1, s).start()

    def start_y(dz):
        for s in SIGNS:
            by(dz, 1, s).start()

    def pass_y(dz):
        for s in SIGNS:
            by_recv(dz, 1, s)
            by(dz, 2, s).start()

    def pass_y_first(k, *js):
        for j in js:
            for s in SIGNS:
                az_recv(k, s, j)
                if k < 4:
                    az(k + 1, s, j).start()

    def arrive(dz):
        for s in SIGNS:
            by_recv(dz, 2, s)

    def take_tokens():
        own_tok.wait()
        gain_load.wait()
        copy(tok, tokbuf.at[1 - c], tok_sem.at[1], tok_sem.at[2], sibling).wait_recv()

    def open_a():
        for s in SIGNS:
            ay_recv(1, s)
            ay(2, s).start()
        pass_z_first(1)
        for j in (1, 2):
            for s in SIGNS:
                az(1, s, j).start()
        start_y(1)

    def close_a():
        for s in SIGNS:
            ay_recv(2, s)
        for s in SIGNS:
            az(1, s, 3).start()

    pieces = [
        (WHOLE, 0, [open_a, scale_rows, lambda: pass_y(0), lambda: start_y(-1), close_a], [lambda: pass_z_first(2), take_tokens, lambda: arrive(0)]),
        (PAIR, 1, [lambda: pass_y(1), lambda: start_y(2)], [lambda: pass_y_first(1, 0, 1, 2, 3)]),
        (LAST, 1, [lambda: pass_y(-1), lambda: start_y(-2)], [lambda: arrive(1)]),
        (LAST, 2, [lambda: pass_z_first(3), lambda: pass_y(2), lambda: start_y(3), pass_scales], [lambda: arrive(-1)]),
        (LAST, 3, [lambda: pass_y(-2), lambda: start_y(-3), lambda: pass_y_first(2, 0, 1)], [lambda: arrive(2)]),
        (PAIR, 3, [], [lambda: pass_y_first(2, 2, 3)]),
        (LAST, 4, [lambda: pass_z_first(4), lambda: pass_y(3), lambda: start_y(4), swap_scales], [lambda: arrive(-2)]),
        (LAST, 5, [lambda: pass_y(-3), lambda: pass_y_first(3, 0, 1)], [lambda: arrive(3)]),
        (PAIR, 5, [take_scales], [lambda: pass_y_first(3, 2, 3)]),
        (LAST, 6, [lambda: pass_y(4)], [lambda: arrive(-3)]),
        (WHOLE, 7, [lambda: pass_y_first(4, 0, 1, 2, 3)], [lambda: arrive(4)]),
    ]

    def look_up(p, column):
        value = jnp.int32(pieces[0][column])
        for i in range(1, len(pieces)):
            value = jnp.where(p == i, pieces[i][column], value)
        return value

    def in_turn(p, column):
        for i, piece in enumerate(pieces):
            if piece[column]:
                @pl.when(p == i)
                def _():
                    for act in piece[column]:
                        act()

    def by_kind(p, run):
        kind, g = look_up(p, 0), look_up(p, 1)
        pl.when(kind == WHOLE)(lambda: run([(g, WHOLE)]))
        pl.when(kind == PAIR)(lambda: run([(g, FIRST), (g + 1, FIRST)]))
        pl.when(kind == LAST)(lambda: run([(g, LAST)]))

    def z_of(g):
        dz = jnp.where(lax.rem(g, 2) == 1, lax.div(g + 1, 2), -lax.div(g, 2))
        return lax.rem(z - dz + NZ, NZ)

    starts, lengths = {FIRST: 0, LAST: SPLIT, WHOLE: 0}, {FIRST: SPLIT, LAST: ROWS - SPLIT, WHOLE: ROWS}

    def rows_of(part):
        return pl.ds(starts[part], lengths[part])

    def place(zz, core, part):
        return pl.ds(pl.multiple_of(zz * (2 * ROWS) + core * ROWS + starts[part], 16), lengths[part])

    def send(g, part, i):
        zz = z_of(g)
        rows = rows_of(part)
        here = place(zz, c, part)
        k = part % 2
        src, dst, recv_sem, dev = (
            lambda: (pbuf.at[g, at_x(2), 0, rows], inc.at[g, 0, rows], r_inc.at[g, k, 0], device(dx=-1)),
            lambda: (pbuf.at[g, at_x(2), 1, rows], inc.at[g, 1, rows], r_inc.at[g, k, 1], device(dx=1)),
            lambda: (pbuf.at[g, at_x(-1), 1, rows], fin.at[0, here], r_fin.at[0, g, c, k], x_dev[-1, 1]),
            lambda: (pbuf.at[g, at_x(1), 0, rows], fin.at[1, here], r_fin.at[1, g, c, k], x_dev[1, 0]),
            lambda: (pbuf.at[g, x, 1 - c, rows], fin.at[2, here], r_sib.at[g, k], sibling),
            lambda: (rel.at[g, 0, rows], fin.at[0, here], r_fin.at[0, g, c, k], x_dev[-1, 0]),
            lambda: (rel.at[g, 1, rows], fin.at[1, here], r_fin.at[1, g, c, k], x_dev[1, 1]),
        )[i]()
        return copy(src, dst, s_x.at[g, k, i], recv_sem, dev)

    def multiply(blocks):
        taken = [wbuf[z_of(g), :, rows_of(part)].reshape(-1, KS) for g, part in blocks]
        rows = taken[0] if len(taken) == 1 else jnp.concatenate(taken)
        for half, sends in ((0, (0, 3)), (1, (1, 2))):
            product = lax.dot_general(
                rows, tokbuf[half], (((1,), (1,)), ((), ())), preferred_element_type=jnp.float32
            ).astype(jnp.bfloat16)
            for n, (g, part) in enumerate(blocks):
                size = NY * lengths[part]
                block = product[n * size:(n + 1) * size]
                pbuf[g, :, half, rows_of(part)] = block.reshape(NY, lengths[part], TOK)
            for i in sends:
                for g, part in blocks:
                    send(g, part, i).start()
        for g, part in blocks:
            send(g, part, 4).start()
        for g, part in blocks:
            fin[2, place(z_of(g), c, part)] = pbuf[g, x, c, rows_of(part)]

    def relay(blocks):
        for g, part in blocks:
            rows = rows_of(part)
            for i, owner in ((0, at_x(-1)), (1, at_x(1))):
                send(g, part, i).wait_recv()
                mixed = pbuf[g, owner, i, rows].astype(jnp.float32) + inc[g, i, rows].astype(jnp.float32)
                rel[g, i, rows] = mixed.astype(jnp.bfloat16)
                send(g, part, 5 + i).start()

    @pl.loop(0, len(pieces))
    def _(p):
        in_turn(p, 2)
        in_turn(p, 3)
        by_kind(p, multiply)

        @pl.when(p > 0)
        def _():
            by_kind(p - 1, relay)

    def each_block(first, last, run):
        @pl.loop(max(first, 1), min(last, 7))
        def _(g):
            run(g, FIRST)
            run(g, LAST)

        for g in (0, 7):
            if first <= g < last:
                run(g, WHOLE)

    def summed(g, part):
        for core in (0, 1):
            for i in (0, 1):
                slot = fin.at[i, place(z_of(g), core, part)]
                copy(slot, slot, s_x.at[0, 0, 0], r_fin.at[i, g, core, part % 2], sibling).wait_recv()
        slot = fin.at[2, place(z_of(g), 1 - c, part)]
        copy(slot, slot, s_x.at[0, 0, 0], r_sib.at[g, part % 2], sibling).wait_recv()

    heads = COLS // HD
    behind = lax.div(at_z(5) * (2 * ROWS) + HD - 1, HD)

    def finish(i):
        h = lax.rem(behind + i, heads)
        rows = pl.ds(pl.multiple_of(h * HD, HD), HD)
        proj = (fin[0, rows].astype(jnp.float32) + fin[1, rows].astype(jnp.float32)) + fin[2, rows].astype(jnp.float32)
        proj = proj * columns[rows, 0:1]
        mean_sq = jnp.sum(proj * proj, axis=0, keepdims=True) / HD
        is_qk = x * heads + h < (QR + KR) // HD
        factor = jnp.where(is_qk, 1.0 / jnp.sqrt(mean_sq + norm_eps), 1.0 / math.sqrt(D))
        out[:, rows] = ((proj * factor).T * gain[rows].reshape(1, HD)).astype(jnp.bfloat16)

    def sent(g, part):
        for i in range(7):
            send(g, part, i).wait_send()

    def sent_before():
        for store in stores():
            store.wait()
        for d in (1, 2, 3):
            sq_copy(d, x).wait_send()
            near_copy(d, y).wait_send()
        for d in range(1, NZ):
            far_copy(d).wait_send()
        swap(c).wait_send()
        tok_out.wait_send()
        for s in SIGNS:
            for hop in (1, 2):
                ay(hop, s).wait_send()
            for k in range(1, 5):
                bz(k, s).wait_send()
                for j in range(4):
                    az(k, s, j).wait_send()
            for dz in (0, 1, -1, 2, -2, 3, -3, 4):
                for hop in (1, 2):
                    by(dz, hop, s).wait_send()
        each_block(0, 6, sent)

    each_block(0, 6, summed)
    pl.loop(0, 6)(finish)
    relay([(7, WHOLE)])
    sent_before()
    each_block(6, 8, summed)
    pl.loop(6, heads)(finish)
    each_block(6, 8, sent)


def body(tokens, qkv_weight, grad, adam_m, adam_v, head_gain):
    dma = pltpu.SemaphoreType.DMA
    anywhere = pl.BlockSpec(memory_space=pl.ANY)
    state = jax.ShapeDtypeStruct((ROWS, KS), jnp.float32)
    vmem = pl.BlockSpec(memory_space=pltpu.VMEM)
    bf16 = jnp.bfloat16
    qkv, new_weight, new_m, new_v = pl.pallas_call(
        kernel,
        out_shape=(
            jax.ShapeDtypeStruct((TOK, COLS), bf16),
            state, state, state,
        ),
        in_specs=[pl.BlockSpec(memory_space=pltpu.HBM)] * 6,
        out_specs=(vmem, anywhere, anywhere, anywhere),
        scratch_shapes=[
            pltpu.VMEM((4, ROWS, KS), jnp.float32),
            pltpu.VMEM((NZ, NY, ROWS, KS), bf16),
            pltpu.VMEM((2, TOK, KS), bf16),
            pltpu.VMEM((8, NX, 2, ROWS, TOK), bf16),
            pltpu.VMEM((8, 2, ROWS, TOK), bf16),
            pltpu.VMEM((8, 2, ROWS, TOK), bf16),
            pltpu.VMEM((3, COLS, TOK), bf16),
            pltpu.VMEM((NX, ROWS, 128), jnp.float32),
            pltpu.VMEM((128, 128), jnp.float32),
            pltpu.VMEM((NY, 8, 128), jnp.float32),
            pltpu.VMEM((2, NZ, 8, 128), jnp.float32),
            pltpu.VMEM((COLS, 128), jnp.float32),
            pltpu.VMEM((COLS,), jnp.float32),
            dma((2, 2)), dma((2, 2)),
            dma((4, 2, 4)), dma((4, 2, 4)),
            dma((4, 2)), dma((4, 2)),
            dma((8, 2, 2)), dma((8, 2, 2)),
            dma((8, 2, 7)), dma((8, 2, 2)), dma((2, 8, 2, 2)), dma((8, 2)),
            dma((3,)), dma((3,)), dma((3,)), dma((3,)), dma((7,)), dma((7,)), dma((2,)), dma((1,)), dma((3,)), dma((ROWS // 16, 4)), dma((4,)),
        ],
        compiler_params=pltpu.CompilerParams(
            collective_id=0, has_side_effects=True, vmem_limit_bytes=52 * 2**20
        ),
        cost_estimate=pl.CostEstimate(
            flops=2 * 2 * TOK * KS * NZ * NY * ROWS, bytes_accessed=4 * 2**20, transcendentals=0
        ),
    )(tokens, qkv_weight, grad, adam_m, adam_v, head_gain)
    return (new_weight, new_m, new_v, qkv)


def solution(mesh):
    return jax.shard_map(
        body,
        mesh=mesh,
        in_specs=(
            P("dp", "hidden"),
            P("dp", "hidden"),
            P("dp", "hidden"),
            P("dp", "hidden"),
            P("dp", "hidden"),
            P("hidden"),
        ),
        out_specs=(P("dp", "hidden"), P("dp", "hidden"), P("dp", "hidden"), P("dp", "hidden")),
        check_vma=False,
    )
```

```python
import math

import jax
import jax.numpy as jnp
from jax import lax
from jax.experimental import pallas as pl
from jax.experimental.pallas import tpu as pltpu
from jax.sharding import PartitionSpec as P

D = 8192
HD = 128
QR = 4096
KR = 512

NY, NZ, NX = 4, 8, 4
ROWS = 80
SPLIT = 32
KS = 2048
TOK = 512
COLS = 1280
HALF = KS // 2

beta_one = 0.9
beta_two = 0.95
learn_rate = 0.05
adam_eps = 1e-08
norm_eps = 1e-06
bias_one = 0.999973438601112
bias_two = 0.994079470779667

MESH = pl.DeviceIdType.MESH
FIRST, LAST, WHOLE, PAIR = 0, 1, 2, 3
SIGNS = (1, -1)


def side(s):
    return 0 if s > 0 else 1


def group_of(dz):
    if dz == 0:
        return 0
    if dz == 4:
        return 7
    return 2 * dz - 1 if dz > 0 else -2 * dz


def kernel(
    tok, weight, grad, adam_m, adam_v, head_gain, out, weight_out, m_out, v_out,
    state, wbuf, tokbuf, pbuf, inc, rel, fin, sq, pad, near, scales, columns, gain,
    s_ay, r_ay, s_az, r_az, s_bz, r_bz, s_by, r_by,
    s_x, r_inc, r_fin, r_sib, s_sq, r_sq, s_near, r_near, s_far, r_far, swap_sem, gain_sem, tok_sem, load_sem, state_sem,
):
    dp = lax.axis_index("dp")
    x = lax.axis_index("hidden")
    y = lax.div(dp, 16)
    z = lax.rem(lax.div(dp, 2), NZ)
    c = lax.rem(dp, 2)

    def device(dy=0, dz=0, dx=0, core=None):
        yy = lax.rem(y + dy + NY, NY)
        zz = lax.rem(z + dz + NZ, NZ)
        return ((yy * NZ + zz) * 2 + (c if core is None else core), lax.rem(x + dx + NX, NX))

    def at_y(dy):
        return lax.rem(y + dy + NY, NY)

    def at_z(dz):
        return lax.rem(z + dz + NZ, NZ)

    def at_x(dx):
        return lax.rem(x + dx + NX, NX)

    y_dev = {s: device(dy=s) for s in SIGNS}
    z_dev = {s: device(dz=s) for s in SIGNS}
    x_dev = {(s, k): device(dx=s, core=k) for s in SIGNS for k in (0, 1)}
    x_two = device(dx=2)
    sibling = device(core=1 - c)

    barrier = pltpu.get_barrier_semaphore()
    partners = list(y_dev.values()) + list(z_dev.values()) + list(x_dev.values()) + [x_two, sibling]
    y_two = device(dy=2)
    z_far = {d: device(dz=d) for d in range(2, NZ - 1)}
    partners += [y_two] + list(z_far.values())
    for partner in partners:
        pl.semaphore_signal(barrier, inc=1, device_id=partner, device_id_type=MESH)

    def copy(src, dst, send_sem, recv_sem, dev):
        return pltpu.make_async_remote_copy(
            src_ref=src, dst_ref=dst, send_sem=send_sem, recv_sem=recv_sem,
            device_id=dev, device_id_type=MESH,
        )

    def load(i, n):
        rows = pl.ds(pl.multiple_of(i * 16, 16), 16)
        src = (grad, adam_m, adam_v, weight)[n]
        return pltpu.make_async_copy(src.at[rows], state.at[n, rows], load_sem.at[i, n])

    for i in range(ROWS // 16):
        for n in range(4):
            load(i, n).start()
    own_tok = pltpu.make_async_copy(tok, tokbuf.at[c], tok_sem.at[0])
    own_tok.start()
    gain_load = pltpu.make_async_copy(head_gain, gain, gain_sem.at[0])
    gain_load.start()

    def adam(i):
        for n in range(4):
            load(i, n).wait()
        rows = pl.ds(pl.multiple_of(i * 16, 16), 16)
        g = state[0, rows]
        new_m = beta_one * state[1, rows] + (1.0 - beta_one) * g
        new_v = beta_two * state[2, rows] + (1.0 - beta_two) * g * g
        step = (learn_rate / bias_one) * new_m / (jnp.sqrt((1.0 / bias_two) * new_v) + adam_eps)
        updated = state[3, rows] - step
        state[1, rows] = new_m
        state[2, rows] = new_v
        state[3, rows] = updated
        wbuf[z, y, rows] = updated.astype(jnp.bfloat16)
        squares = updated * updated
        part = squares[:, 0:128]
        for k in range(1, KS // 128):
            part = part + squares[:, k * 128:(k + 1) * 128]
        sq[x, rows] = part

    pl.loop(0, SPLIT // 16)(adam)
    pl.semaphore_wait(barrier, len(partners))

    def part_a(zz, yy, s=None):
        ref = wbuf.at[zz, yy, pl.ds(0, SPLIT)]
        return ref if s is None else ref.at[:, pl.ds(side(s) * HALF, HALF)]

    def part_b(zz, yy, s=None):
        ref = wbuf.at[zz, yy, pl.ds(SPLIT, ROWS - SPLIT)]
        return ref if s is None else ref.at[:, pl.ds(side(s) * HALF, HALF)]

    y_order = (0, -1, 1, 2)

    def ay(hop, s):
        if hop == 1:
            ref = part_a(z, y)
        else:
            ref = part_a(z, at_y(-s), s)
        return copy(ref, ref, s_ay.at[hop - 1, side(s)], r_ay.at[hop - 1, side(s)], y_dev[s])

    def ay_recv(hop, s):
        ref = part_a(z, at_y(-s)) if hop == 1 else part_a(z, at_y(-2 * s), s)
        copy(ref, ref, s_ay.at[hop - 1, side(s)], r_ay.at[hop - 1, side(s)], y_dev[s]).wait_recv()

    def az(k, s, j):
        ref = part_a(at_z(-(k - 1) * s), at_y(y_order[j]), s if k == 4 else None)
        return copy(ref, ref, s_az.at[k - 1, side(s), j], r_az.at[k - 1, side(s), j], z_dev[s])

    def az_recv(k, s, j):
        ref = part_a(at_z(-k * s), at_y(y_order[j]), s if k == 4 else None)
        copy(ref, ref, s_az.at[k - 1, side(s), j], r_az.at[k - 1, side(s), j], z_dev[s]).wait_recv()

    def bz(k, s):
        ref = part_b(at_z(-(k - 1) * s), y, s if k == 4 else None)
        return copy(ref, ref, s_bz.at[k - 1, side(s)], r_bz.at[k - 1, side(s)], z_dev[s])

    def bz_recv(k, s):
        ref = part_b(at_z(-k * s), y, s if k == 4 else None)
        copy(ref, ref, s_bz.at[k - 1, side(s)], r_bz.at[k - 1, side(s)], z_dev[s]).wait_recv()

    def by(dz, hop, s):
        g = group_of(dz)
        ref = part_b(at_z(-dz), y) if hop == 1 else part_b(at_z(-dz), at_y(-s), s)
        return copy(ref, ref, s_by.at[g, hop - 1, side(s)], r_by.at[g, hop - 1, side(s)], y_dev[s])

    def by_recv(dz, hop, s):
        g = group_of(dz)
        ref = part_b(at_z(-dz), at_y(-s)) if hop == 1 else part_b(at_z(-dz), at_y(-2 * s), s)
        copy(ref, ref, s_by.at[g, hop - 1, side(s)], r_by.at[g, hop - 1, side(s)], y_dev[s]).wait_recv()

    for s in SIGNS:
        ay(1, s).start()
    pl.loop(SPLIT // 16, ROWS // 16)(adam)
    for s in SIGNS:
        bz(1, s).start()
        by(0, 1, s).start()
    for s in SIGNS:
        az(1, s, 0).start()

    sq_dev = {1: device(dx=1), 2: x_two, 3: device(dx=3)}

    def sq_copy(d, slot):
        return copy(sq.at[slot], sq.at[slot], s_sq.at[d - 1], r_sq.at[d - 1], sq_dev[d])

    for d in (2, 1, 3):
        sq_copy(d, x).start()
    tok_out = copy(tok, tokbuf.at[c], tok_sem.at[1], tok_sem.at[2], sibling)
    tok_out.start()

    def stores():
        return [
            pltpu.make_async_copy(state.at[i], dst, state_sem.at[i])
            for i, dst in ((1, m_out), (2, v_out), (3, weight_out))
        ]

    def scale_rows():
        for d in (1, 2, 3):
            sq_copy(d, at_x(-d)).wait_recv()
        total = jnp.sum(sq[0] + sq[1] + sq[2] + sq[3], axis=1, keepdims=True)
        row_scale = 1.0 / jnp.sqrt(total / D + norm_eps)
        pad[...] = jnp.ones_like(pad)
        pad[0:ROWS] = jnp.broadcast_to(row_scale, (ROWS, 128))
        near[y] = pad[...].T[0:8]
        for d in (1, 2, 3):
            near_copy(d, y).start()
        state[3] = state[3] * row_scale
        for store in stores():
            store.start()

    def near_copy(d, slot):
        dev = y_two if d == 2 else y_dev[1 if d == 1 else -1]
        return copy(near.at[slot], near.at[slot], s_near.at[d - 1], r_near.at[d - 1], dev)

    def far_copy(d):
        dev = z_far[d] if d in z_far else z_dev[1 if d == 1 else -1]
        return copy(near.at[x], scales.at[c, z], s_far.at[d - 1], r_far.at[d - 1], dev)

    def far_recv(d):
        slot = scales.at[c, at_z(-d)]
        copy(slot, slot, s_far.at[d - 1], r_far.at[d - 1], sibling).wait_recv()

    def swap(core):
        return copy(scales.at[core], scales.at[core], swap_sem.at[0], swap_sem.at[1], sibling)

    def pass_scales():
        for d in (1, 2, 3):
            near_copy(d, at_y(-d)).wait_recv()
        scales[c, z] = near[x]
        for d in range(1, NZ):
            far_copy(d).start()

    def swap_scales():
        for d in range(1, NZ):
            far_recv(d)
        swap(c).start()

    def take_scales():
        swap(1 - c).wait_recv()

        @pl.loop(0, NZ)
        def _(zz):
            for core in (0, 1):
                turned = jnp.broadcast_to(scales[core, zz, 0:1], (128, 128)).T
                columns[pl.ds(pl.multiple_of(zz * (2 * ROWS) + core * ROWS, 16), ROWS)] = turned[0:ROWS]

    def pass_z_first(k):
        for s in SIGNS:
            bz_recv(k, s)
            if k < 4:
                bz(k + 1, s).start()

    def start_y(dz):
        for s in SIGNS:
            by(dz, 1, s).start()

    def pass_y(dz):
        for s in SIGNS:
            by_recv(dz, 1, s)
            by(dz, 2, s).start()

    def pass_y_first(k, *js):
        for j in js:
            for s in SIGNS:
                az_recv(k, s, j)
                if k < 4:
                    az(k + 1, s, j).start()

    def arrive(dz):
        for s in SIGNS:
            by_recv(dz, 2, s)

    def take_tokens():
        own_tok.wait()
        gain_load.wait()
        copy(tok, tokbuf.at[1 - c], tok_sem.at[1], tok_sem.at[2], sibling).wait_recv()

    def open_a():
        for s in SIGNS:
            ay_recv(1, s)
            ay(2, s).start()
        pass_z_first(1)
        for j in (1, 2):
            for s in SIGNS:
                az(1, s, j).start()
        start_y(1)

    def close_a():
        for s in SIGNS:
            ay_recv(2, s)
        for s in SIGNS:
            az(1, s, 3).start()

    pieces = [
        (WHOLE, 0, [open_a, lambda: pass_y(0), lambda: start_y(-1), close_a], [lambda: pass_z_first(2), take_tokens, lambda: arrive(0)]),
        (PAIR, 1, [lambda: pass_y(1), lambda: start_y(2), scale_rows], [lambda: pass_y_first(1, 0, 1, 2, 3)]),
        (LAST, 1, [lambda: pass_y(-1), lambda: start_y(-2)], [lambda: arrive(1)]),
        (LAST, 2, [lambda: pass_z_first(3), lambda: pass_y(2), lambda: start_y(3), pass_scales], [lambda: arrive(-1)]),
        (LAST, 3, [lambda: pass_y(-2), lambda: start_y(-3), lambda: pass_y_first(2, 0, 1)], [lambda: arrive(2)]),
        (PAIR, 3, [], [lambda: pass_y_first(2, 2, 3)]),
        (LAST, 4, [lambda: pass_z_first(4), lambda: pass_y(3), lambda: start_y(4), swap_scales], [lambda: arrive(-2)]),
        (LAST, 5, [lambda: pass_y(-3), lambda: pass_y_first(3, 0, 1)], [lambda: arrive(3)]),
        (PAIR, 5, [take_scales], [lambda: pass_y_first(3, 2, 3)]),
        (LAST, 6, [lambda: pass_y(4)], [lambda: arrive(-3)]),
        (WHOLE, 7, [lambda: pass_y_first(4, 0, 1, 2, 3)], [lambda: arrive(4)]),
    ]

    def look_up(p, column):
        value = jnp.int32(pieces[0][column])
        for i in range(1, len(pieces)):
            value = jnp.where(p == i, pieces[i][column], value)
        return value

    def in_turn(p, column):
        for i, piece in enumerate(pieces):
            if piece[column]:
                @pl.when(p == i)
                def _():
                    for act in piece[column]:
                        act()

    def by_kind(p, run):
        kind, g = look_up(p, 0), look_up(p, 1)
        pl.when(kind == WHOLE)(lambda: run([(g, WHOLE)]))
        pl.when(kind == PAIR)(lambda: run([(g, FIRST), (g + 1, FIRST)]))
        pl.when(kind == LAST)(lambda: run([(g, LAST)]))

    def z_of(g):
        dz = jnp.where(lax.rem(g, 2) == 1, lax.div(g + 1, 2), -lax.div(g, 2))
        return lax.rem(z - dz + NZ, NZ)

    starts, lengths = {FIRST: 0, LAST: SPLIT, WHOLE: 0}, {FIRST: SPLIT, LAST: ROWS - SPLIT, WHOLE: ROWS}

    def rows_of(part):
        return pl.ds(starts[part], lengths[part])

    def place(zz, core, part):
        return pl.ds(pl.multiple_of(zz * (2 * ROWS) + core * ROWS + starts[part], 16), lengths[part])

    def send(g, part, i):
        zz = z_of(g)
        rows = rows_of(part)
        here = place(zz, c, part)
        k = part % 2
        src, dst, recv_sem, dev = (
            lambda: (pbuf.at[g, at_x(2), 0, rows], inc.at[g, 0, rows], r_inc.at[g, k, 0], device(dx=-1)),
            lambda: (pbuf.at[g, at_x(2), 1, rows], inc.at[g, 1, rows], r_inc.at[g, k, 1], device(dx=1)),
            lambda: (pbuf.at[g, at_x(-1), 1, rows], fin.at[0, here], r_fin.at[0, g, c, k], x_dev[-1, 1]),
            lambda: (pbuf.at[g, at_x(1), 0, rows], fin.at[1, here], r_fin.at[1, g, c, k], x_dev[1, 0]),
            lambda: (pbuf.at[g, x, 1 - c, rows], fin.at[2, here], r_sib.at[g, k], sibling),
            lambda: (rel.at[g, 0, rows], fin.at[0, here], r_fin.at[0, g, c, k], x_dev[-1, 0]),
            lambda: (rel.at[g, 1, rows], fin.at[1, here], r_fin.at[1, g, c, k], x_dev[1, 1]),
        )[i]()
        return copy(src, dst, s_x.at[g, k, i], recv_sem, dev)

    def multiply(blocks):
        taken = [wbuf[z_of(g), :, rows_of(part)].reshape(-1, KS) for g, part in blocks]
        rows = taken[0] if len(taken) == 1 else jnp.concatenate(taken)
        product = lax.dot_general(
            rows, tokbuf[...].reshape(2 * TOK, KS), (((1,), (1,)), ((), ())), preferred_element_type=jnp.float32
        ).astype(jnp.bfloat16)
        for n, (g, part) in enumerate(blocks):
            size = NY * lengths[part]
            for half in (0, 1):
                block = product[n * size:(n + 1) * size, half * TOK:(half + 1) * TOK]
                pbuf[g, :, half, rows_of(part)] = block.reshape(NY, lengths[part], TOK)
        for i in range(5):
            for g, part in blocks:
                send(g, part, i).start()
        for g, part in blocks:
            fin[2, place(z_of(g), c, part)] = pbuf[g, x, c, rows_of(part)]

    def relay(blocks):
        for g, part in blocks:
            rows = rows_of(part)
            for i, owner in ((0, at_x(-1)), (1, at_x(1))):
                send(g, part, i).wait_recv()
                mixed = pbuf[g, owner, i, rows].astype(jnp.float32) + inc[g, i, rows].astype(jnp.float32)
                rel[g, i, rows] = mixed.astype(jnp.bfloat16)
                send(g, part, 5 + i).start()

    @pl.loop(0, len(pieces))
    def _(p):
        in_turn(p, 2)
        in_turn(p, 3)
        by_kind(p, multiply)

        @pl.when(p > 0)
        def _():
            by_kind(p - 1, relay)

    def each_block(first, last, run):
        @pl.loop(max(first, 1), min(last, 7))
        def _(g):
            run(g, FIRST)
            run(g, LAST)

        for g in (0, 7):
            if first <= g < last:
                run(g, WHOLE)

    def summed(g, part):
        for core in (0, 1):
            for i in (0, 1):
                slot = fin.at[i, place(z_of(g), core, part)]
                copy(slot, slot, s_x.at[0, 0, 0], r_fin.at[i, g, core, part % 2], sibling).wait_recv()
        slot = fin.at[2, place(z_of(g), 1 - c, part)]
        copy(slot, slot, s_x.at[0, 0, 0], r_sib.at[g, part % 2], sibling).wait_recv()

    heads = COLS // HD
    behind = lax.div(at_z(5) * (2 * ROWS) + HD - 1, HD)

    def finish(i):
        h = lax.rem(behind + i, heads)
        rows = pl.ds(pl.multiple_of(h * HD, HD), HD)
        proj = (fin[0, rows].astype(jnp.float32) + fin[1, rows].astype(jnp.float32)) + fin[2, rows].astype(jnp.float32)
        proj = proj * columns[rows, 0:1]
        mean_sq = jnp.sum(proj * proj, axis=0, keepdims=True) / HD
        is_qk = x * heads + h < (QR + KR) // HD
        factor = jnp.where(is_qk, 1.0 / jnp.sqrt(mean_sq + norm_eps), 1.0 / math.sqrt(D))
        out[:, rows] = ((proj * factor).T * gain[rows].reshape(1, HD)).astype(jnp.bfloat16)

    def sent(g, part):
        for i in range(7):
            send(g, part, i).wait_send()

    def sent_before():
        for store in stores():
            store.wait()
        for d in (1, 2, 3):
            sq_copy(d, x).wait_send()
            near_copy(d, y).wait_send()
        for d in range(1, NZ):
            far_copy(d).wait_send()
        swap(c).wait_send()
        tok_out.wait_send()
        for s in SIGNS:
            for hop in (1, 2):
                ay(hop, s).wait_send()
            for k in range(1, 5):
                bz(k, s).wait_send()
                for j in range(4):
                    az(k, s, j).wait_send()
            for dz in (0, 1, -1, 2, -2, 3, -3, 4):
                for hop in (1, 2):
                    by(dz, hop, s).wait_send()
        each_block(0, 6, sent)

    each_block(0, 6, summed)
    pl.loop(0, 6)(finish)
    relay([(7, WHOLE)])
    sent_before()
    each_block(6, 8, summed)
    pl.loop(6, heads)(finish)
    each_block(6, 8, sent)


def hand_over_kernel(*refs):
    results, outputs, held, load_sem, store_sem = refs[0:4], refs[4:8], refs[8:12], refs[12], refs[13]
    loads = [pltpu.make_async_copy(results[i], held[i], load_sem.at[i]) for i in range(4)]
    stores = [pltpu.make_async_copy(held[i], outputs[i], store_sem.at[i]) for i in range(4)]
    for load in loads:
        load.start()
    for load, store in zip(loads, stores):
        load.wait()
        store.start()
    for store in stores:
        store.wait()


def hand_over(*arrays):
    return pl.pallas_call(
        hand_over_kernel,
        out_shape=[jax.ShapeDtypeStruct(a.shape, a.dtype) for a in arrays],
        in_specs=[pl.BlockSpec(memory_space=pl.ANY)] * 4,
        out_specs=[pl.BlockSpec(memory_space=pl.ANY)] * 4,
        scratch_shapes=[pltpu.VMEM(a.shape, a.dtype) for a in arrays]
        + [pltpu.SemaphoreType.DMA((4,)), pltpu.SemaphoreType.DMA((4,))],
        compiler_params=pltpu.CompilerParams(vmem_limit_bytes=60 * 2**20),
    )(*arrays)


def body(tokens, qkv_weight, grad, adam_m, adam_v, head_gain):
    dma = pltpu.SemaphoreType.DMA
    anywhere = pl.BlockSpec(memory_space=pl.ANY)
    state = jax.ShapeDtypeStruct((ROWS, KS), jnp.float32)
    vmem = pl.BlockSpec(memory_space=pltpu.VMEM)
    bf16 = jnp.bfloat16
    qkv, new_weight, new_m, new_v = pl.pallas_call(
        kernel,
        out_shape=(
            jax.ShapeDtypeStruct((TOK, COLS), bf16),
            state, state, state,
        ),
        in_specs=[pl.BlockSpec(memory_space=pltpu.HBM)] * 6,
        out_specs=(vmem, anywhere, anywhere, anywhere),
        scratch_shapes=[
            pltpu.VMEM((4, ROWS, KS), jnp.float32),
            pltpu.VMEM((NZ, NY, ROWS, KS), bf16),
            pltpu.VMEM((2, TOK, KS), bf16),
            pltpu.VMEM((8, NX, 2, ROWS, TOK), bf16),
            pltpu.VMEM((8, 2, ROWS, TOK), bf16),
            pltpu.VMEM((8, 2, ROWS, TOK), bf16),
            pltpu.VMEM((3, COLS, TOK), bf16),
            pltpu.VMEM((NX, ROWS, 128), jnp.float32),
            pltpu.VMEM((128, 128), jnp.float32),
            pltpu.VMEM((NY, 8, 128), jnp.float32),
            pltpu.VMEM((2, NZ, 8, 128), jnp.float32),
            pltpu.VMEM((COLS, 128), jnp.float32),
            pltpu.VMEM((COLS,), jnp.float32),
            dma((2, 2)), dma((2, 2)),
            dma((4, 2, 4)), dma((4, 2, 4)),
            dma((4, 2)), dma((4, 2)),
            dma((8, 2, 2)), dma((8, 2, 2)),
            dma((8, 2, 7)), dma((8, 2, 2)), dma((2, 8, 2, 2)), dma((8, 2)),
            dma((3,)), dma((3,)), dma((3,)), dma((3,)), dma((7,)), dma((7,)), dma((2,)), dma((1,)), dma((3,)), dma((ROWS // 16, 4)), dma((4,)),
        ],
        compiler_params=pltpu.CompilerParams(
            collective_id=0, has_side_effects=True, vmem_limit_bytes=60 * 2**20
        ),
        cost_estimate=pl.CostEstimate(
            flops=2 * 2 * TOK * KS * NZ * NY * ROWS, bytes_accessed=4 * 2**20, transcendentals=0
        ),
    )(tokens, qkv_weight, grad, adam_m, adam_v, head_gain)
    return hand_over(new_weight, new_m, new_v, qkv)


def solution(mesh):
    return jax.shard_map(
        body,
        mesh=mesh,
        in_specs=(
            P("dp", "hidden"),
            P("dp", "hidden"),
            P("dp", "hidden"),
            P("dp", "hidden"),
            P("dp", "hidden"),
            P("hidden"),
        ),
        out_specs=(P("dp", "hidden"), P("dp", "hidden"), P("dp", "hidden"), P("dp", "hidden")),
        check_vma=False,
    )
```

```python
import math

import jax
import jax.numpy as jnp
from jax import lax
from jax.experimental import pallas as pl
from jax.experimental.pallas import tpu as pltpu
from jax.sharding import PartitionSpec as P

D = 8192
HD = 128
QR = 4096
KR = 512

NY, NZ, NX = 4, 8, 4
ROWS = 80
SPLIT = 32
KS = 2048
TOK = 512
COLS = 1280
HALF = KS // 2

beta_one = 0.9
beta_two = 0.95
learn_rate = 0.05
adam_eps = 1e-08
norm_eps = 1e-06
bias_one = 0.999973438601112
bias_two = 0.994079470779667

MESH = pl.DeviceIdType.MESH
FIRST, LAST, WHOLE, PAIR = 0, 1, 2, 3
SIGNS = (1, -1)


def side(s):
    return 0 if s > 0 else 1


def group_of(dz):
    if dz == 0:
        return 0
    if dz == 4:
        return 7
    return 2 * dz - 1 if dz > 0 else -2 * dz


def kernel(
    tok, weight, grad, adam_m, adam_v, head_gain, qkv_out, weight_out, m_out, v_out,
    state, wbuf, tokbuf, pbuf, inc, rel, fin, sq, pad, near, scales, columns, gain, out,
    s_ay, r_ay, s_az, r_az, s_bz, r_bz, s_by, r_by,
    s_x, r_inc, r_fin, r_sib, s_sq, r_sq, s_near, r_near, s_far, r_far, swap_sem, gain_sem, out_sem, tok_sem, load_sem, state_sem,
):
    dp = lax.axis_index("dp")
    x = lax.axis_index("hidden")
    y = lax.div(dp, 16)
    z = lax.rem(lax.div(dp, 2), NZ)
    c = lax.rem(dp, 2)

    def device(dy=0, dz=0, dx=0, core=None):
        yy = lax.rem(y + dy + NY, NY)
        zz = lax.rem(z + dz + NZ, NZ)
        return ((yy * NZ + zz) * 2 + (c if core is None else core), lax.rem(x + dx + NX, NX))

    def at_y(dy):
        return lax.rem(y + dy + NY, NY)

    def at_z(dz):
        return lax.rem(z + dz + NZ, NZ)

    def at_x(dx):
        return lax.rem(x + dx + NX, NX)

    y_dev = {s: device(dy=s) for s in SIGNS}
    z_dev = {s: device(dz=s) for s in SIGNS}
    x_dev = {(s, k): device(dx=s, core=k) for s in SIGNS for k in (0, 1)}
    x_two = device(dx=2)
    sibling = device(core=1 - c)

    barrier = pltpu.get_barrier_semaphore()
    partners = list(y_dev.values()) + list(z_dev.values()) + list(x_dev.values()) + [x_two, sibling]
    y_two = device(dy=2)
    z_far = {d: device(dz=d) for d in range(2, NZ - 1)}
    partners += [y_two] + list(z_far.values())
    for partner in partners:
        pl.semaphore_signal(barrier, inc=1, device_id=partner, device_id_type=MESH)

    def copy(src, dst, send_sem, recv_sem, dev):
        return pltpu.make_async_remote_copy(
            src_ref=src, dst_ref=dst, send_sem=send_sem, recv_sem=recv_sem,
            device_id=dev, device_id_type=MESH,
        )

    def load(i, n):
        rows = pl.ds(pl.multiple_of(i * 16, 16), 16)
        src = (grad, adam_m, adam_v, weight)[n]
        return pltpu.make_async_copy(src.at[rows], state.at[n, rows], load_sem.at[i, n])

    for i in range(ROWS // 16):
        for n in range(4):
            load(i, n).start()
    own_tok = pltpu.make_async_copy(tok, tokbuf.at[c], tok_sem.at[0])
    own_tok.start()
    gain_load = pltpu.make_async_copy(head_gain, gain, gain_sem.at[0])
    gain_load.start()

    def adam(i):
        for n in range(4):
            load(i, n).wait()
        rows = pl.ds(pl.multiple_of(i * 16, 16), 16)
        g = state[0, rows]
        new_m = beta_one * state[1, rows] + (1.0 - beta_one) * g
        new_v = beta_two * state[2, rows] + (1.0 - beta_two) * g * g
        step = (learn_rate / bias_one) * new_m / (jnp.sqrt((1.0 / bias_two) * new_v) + adam_eps)
        updated = state[3, rows] - step
        state[1, rows] = new_m
        state[2, rows] = new_v
        state[3, rows] = updated
        wbuf[z, y, rows] = updated.astype(jnp.bfloat16)
        squares = updated * updated
        part = squares[:, 0:128]
        for k in range(1, KS // 128):
            part = part + squares[:, k * 128:(k + 1) * 128]
        sq[x, rows] = part

    pl.loop(0, SPLIT // 16)(adam)
    pl.semaphore_wait(barrier, len(partners))

    def part_a(zz, yy, s=None):
        ref = wbuf.at[zz, yy, pl.ds(0, SPLIT)]
        return ref if s is None else ref.at[:, pl.ds(side(s) * HALF, HALF)]

    def part_b(zz, yy, s=None):
        ref = wbuf.at[zz, yy, pl.ds(SPLIT, ROWS - SPLIT)]
        return ref if s is None else ref.at[:, pl.ds(side(s) * HALF, HALF)]

    y_order = (0, -1, 1, 2)

    def ay(hop, s):
        if hop == 1:
            ref = part_a(z, y)
        else:
            ref = part_a(z, at_y(-s), s)
        return copy(ref, ref, s_ay.at[hop - 1, side(s)], r_ay.at[hop - 1, side(s)], y_dev[s])

    def ay_recv(hop, s):
        ref = part_a(z, at_y(-s)) if hop == 1 else part_a(z, at_y(-2 * s), s)
        copy(ref, ref, s_ay.at[hop - 1, side(s)], r_ay.at[hop - 1, side(s)], y_dev[s]).wait_recv()

    def az(k, s, j):
        ref = part_a(at_z(-(k - 1) * s), at_y(y_order[j]), s if k == 4 else None)
        return copy(ref, ref, s_az.at[k - 1, side(s), j], r_az.at[k - 1, side(s), j], z_dev[s])

    def az_recv(k, s, j):
        ref = part_a(at_z(-k * s), at_y(y_order[j]), s if k == 4 else None)
        copy(ref, ref, s_az.at[k - 1, side(s), j], r_az.at[k - 1, side(s), j], z_dev[s]).wait_recv()

    def bz(k, s):
        ref = part_b(at_z(-(k - 1) * s), y, s if k == 4 else None)
        return copy(ref, ref, s_bz.at[k - 1, side(s)], r_bz.at[k - 1, side(s)], z_dev[s])

    def bz_recv(k, s):
        ref = part_b(at_z(-k * s), y, s if k == 4 else None)
        copy(ref, ref, s_bz.at[k - 1, side(s)], r_bz.at[k - 1, side(s)], z_dev[s]).wait_recv()

    def by(dz, hop, s):
        g = group_of(dz)
        ref = part_b(at_z(-dz), y) if hop == 1 else part_b(at_z(-dz), at_y(-s), s)
        return copy(ref, ref, s_by.at[g, hop - 1, side(s)], r_by.at[g, hop - 1, side(s)], y_dev[s])

    def by_recv(dz, hop, s):
        g = group_of(dz)
        ref = part_b(at_z(-dz), at_y(-s)) if hop == 1 else part_b(at_z(-dz), at_y(-2 * s), s)
        copy(ref, ref, s_by.at[g, hop - 1, side(s)], r_by.at[g, hop - 1, side(s)], y_dev[s]).wait_recv()

    for s in SIGNS:
        ay(1, s).start()
    pl.loop(SPLIT // 16, ROWS // 16)(adam)
    for s in SIGNS:
        bz(1, s).start()
        by(0, 1, s).start()
    for s in SIGNS:
        az(1, s, 0).start()

    sq_dev = {1: device(dx=1), 2: x_two, 3: device(dx=3)}

    def sq_copy(d, slot):
        return copy(sq.at[slot], sq.at[slot], s_sq.at[d - 1], r_sq.at[d - 1], sq_dev[d])

    for d in (2, 1, 3):
        sq_copy(d, x).start()
    tok_out = copy(tok, tokbuf.at[c], tok_sem.at[1], tok_sem.at[2], sibling)
    tok_out.start()

    def stores():
        return [
            pltpu.make_async_copy(state.at[i], dst, state_sem.at[i])
            for i, dst in ((1, m_out), (2, v_out), (3, weight_out))
        ]

    def scale_rows():
        for d in (1, 2, 3):
            sq_copy(d, at_x(-d)).wait_recv()
        total = jnp.sum(sq[0] + sq[1] + sq[2] + sq[3], axis=1, keepdims=True)
        row_scale = 1.0 / jnp.sqrt(total / D + norm_eps)
        pad[...] = jnp.ones_like(pad)
        pad[0:ROWS] = jnp.broadcast_to(row_scale, (ROWS, 128))
        near[y] = pad[...].T[0:8]
        for d in (1, 2, 3):
            near_copy(d, y).start()
        state[3] = state[3] * row_scale
        for store in stores():
            store.start()

    def near_copy(d, slot):
        dev = y_two if d == 2 else y_dev[1 if d == 1 else -1]
        return copy(near.at[slot], near.at[slot], s_near.at[d - 1], r_near.at[d - 1], dev)

    def far_copy(d):
        dev = z_far[d] if d in z_far else z_dev[1 if d == 1 else -1]
        return copy(near.at[x], scales.at[c, z], s_far.at[d - 1], r_far.at[d - 1], dev)

    def far_recv(d):
        slot = scales.at[c, at_z(-d)]
        copy(slot, slot, s_far.at[d - 1], r_far.at[d - 1], sibling).wait_recv()

    def swap(core):
        return copy(scales.at[core], scales.at[core], swap_sem.at[0], swap_sem.at[1], sibling)

    def pass_scales():
        for d in (1, 2, 3):
            near_copy(d, at_y(-d)).wait_recv()
        scales[c, z] = near[x]
        for d in range(1, NZ):
            far_copy(d).start()

    def swap_scales():
        for d in range(1, NZ):
            far_recv(d)
        swap(c).start()

    def take_scales():
        swap(1 - c).wait_recv()

        @pl.loop(0, NZ)
        def _(zz):
            for core in (0, 1):
                turned = jnp.broadcast_to(scales[core, zz, 0:1], (128, 128)).T
                columns[pl.ds(pl.multiple_of(zz * (2 * ROWS) + core * ROWS, 16), ROWS)] = turned[0:ROWS]

    def pass_z_first(k):
        for s in SIGNS:
            bz_recv(k, s)
            if k < 4:
                bz(k + 1, s).start()

    def start_y(dz):
        for s in SIGNS:
            by(dz, 1, s).start()

    def pass_y(dz):
        for s in SIGNS:
            by_recv(dz, 1, s)
            by(dz, 2, s).start()

    def pass_y_first(k, *js):
        for j in js:
            for s in SIGNS:
                az_recv(k, s, j)
                if k < 4:
                    az(k + 1, s, j).start()

    def arrive(dz):
        for s in SIGNS:
            by_recv(dz, 2, s)

    def take_tokens():
        own_tok.wait()
        gain_load.wait()
        copy(tok, tokbuf.at[1 - c], tok_sem.at[1], tok_sem.at[2], sibling).wait_recv()

    def open_a():
        for s in SIGNS:
            ay_recv(1, s)
            ay(2, s).start()
        pass_z_first(1)
        for j in (1, 2):
            for s in SIGNS:
                az(1, s, j).start()
        start_y(1)

    def close_a():
        for s in SIGNS:
            ay_recv(2, s)
        for s in SIGNS:
            az(1, s, 3).start()

    pieces = [
        (WHOLE, 0, [open_a, lambda: pass_y(0), lambda: start_y(-1), close_a], [lambda: pass_z_first(2), take_tokens, lambda: arrive(0)]),
        (PAIR, 1, [lambda: pass_y(1), lambda: start_y(2), scale_rows], [lambda: pass_y_first(1, 0, 1, 2, 3)]),
        (LAST, 1, [lambda: pass_y(-1), lambda: start_y(-2)], [lambda: arrive(1)]),
        (LAST, 2, [lambda: pass_z_first(3), lambda: pass_y(2), lambda: start_y(3), pass_scales], [lambda: arrive(-1)]),
        (LAST, 3, [lambda: pass_y(-2), lambda: start_y(-3), lambda: pass_y_first(2, 0, 1)], [lambda: arrive(2)]),
        (PAIR, 3, [], [lambda: pass_y_first(2, 2, 3)]),
        (LAST, 4, [lambda: pass_z_first(4), lambda: pass_y(3), lambda: start_y(4), swap_scales], [lambda: arrive(-2)]),
        (LAST, 5, [lambda: pass_y(-3), lambda: pass_y_first(3, 0, 1)], [lambda: arrive(3)]),
        (PAIR, 5, [take_scales], [lambda: pass_y_first(3, 2, 3)]),
        (LAST, 6, [lambda: pass_y(4)], [lambda: arrive(-3)]),
        (WHOLE, 7, [lambda: pass_y_first(4, 0, 1, 2, 3)], [lambda: arrive(4)]),
    ]

    def look_up(p, column):
        value = jnp.int32(pieces[0][column])
        for i in range(1, len(pieces)):
            value = jnp.where(p == i, pieces[i][column], value)
        return value

    def in_turn(p, column):
        for i, piece in enumerate(pieces):
            if piece[column]:
                @pl.when(p == i)
                def _():
                    for act in piece[column]:
                        act()

    def by_kind(p, run):
        kind, g = look_up(p, 0), look_up(p, 1)
        pl.when(kind == WHOLE)(lambda: run([(g, WHOLE)]))
        pl.when(kind == PAIR)(lambda: run([(g, FIRST), (g + 1, FIRST)]))
        pl.when(kind == LAST)(lambda: run([(g, LAST)]))

    def z_of(g):
        dz = jnp.where(lax.rem(g, 2) == 1, lax.div(g + 1, 2), -lax.div(g, 2))
        return lax.rem(z - dz + NZ, NZ)

    starts, lengths = {FIRST: 0, LAST: SPLIT, WHOLE: 0}, {FIRST: SPLIT, LAST: ROWS - SPLIT, WHOLE: ROWS}

    def rows_of(part):
        return pl.ds(starts[part], lengths[part])

    def place(zz, core, part):
        return pl.ds(pl.multiple_of(zz * (2 * ROWS) + core * ROWS + starts[part], 16), lengths[part])

    def send(g, part, i):
        zz = z_of(g)
        rows = rows_of(part)
        here = place(zz, c, part)
        k = part % 2
        src, dst, recv_sem, dev = (
            lambda: (pbuf.at[g, at_x(2), 0, rows], inc.at[g, 0, rows], r_inc.at[g, k, 0], device(dx=-1)),
            lambda: (pbuf.at[g, at_x(2), 1, rows], inc.at[g, 1, rows], r_inc.at[g, k, 1], device(dx=1)),
            lambda: (pbuf.at[g, at_x(-1), 1, rows], fin.at[0, here], r_fin.at[0, g, c, k], x_dev[-1, 1]),
            lambda: (pbuf.at[g, at_x(1), 0, rows], fin.at[1, here], r_fin.at[1, g, c, k], x_dev[1, 0]),
            lambda: (pbuf.at[g, x, 1 - c, rows], fin.at[2, here], r_sib.at[g, k], sibling),
            lambda: (rel.at[g, 0, rows], fin.at[0, here], r_fin.at[0, g, c, k], x_dev[-1, 0]),
            lambda: (rel.at[g, 1, rows], fin.at[1, here], r_fin.at[1, g, c, k], x_dev[1, 1]),
        )[i]()
        return copy(src, dst, s_x.at[g, k, i], recv_sem, dev)

    def multiply(blocks):
        taken = [wbuf[z_of(g), :, rows_of(part)].reshape(-1, KS) for g, part in blocks]
        rows = taken[0] if len(taken) == 1 else jnp.concatenate(taken)
        product = lax.dot_general(
            rows, tokbuf[...].reshape(2 * TOK, KS), (((1,), (1,)), ((), ())), preferred_element_type=jnp.float32
        ).astype(jnp.bfloat16)
        for n, (g, part) in enumerate(blocks):
            size = NY * lengths[part]
            for half in (0, 1):
                block = product[n * size:(n + 1) * size, half * TOK:(half + 1) * TOK]
                pbuf[g, :, half, rows_of(part)] = block.reshape(NY, lengths[part], TOK)
        for i in range(5):
            for g, part in blocks:
                send(g, part, i).start()
        for g, part in blocks:
            fin[2, place(z_of(g), c, part)] = pbuf[g, x, c, rows_of(part)]

    def relay(blocks):
        for g, part in blocks:
            rows = rows_of(part)
            for i, owner in ((0, at_x(-1)), (1, at_x(1))):
                send(g, part, i).wait_recv()
                mixed = pbuf[g, owner, i, rows].astype(jnp.float32) + inc[g, i, rows].astype(jnp.float32)
                rel[g, i, rows] = mixed.astype(jnp.bfloat16)
                send(g, part, 5 + i).start()

    @pl.loop(0, len(pieces))
    def _(p):
        in_turn(p, 2)
        in_turn(p, 3)
        by_kind(p, multiply)

        @pl.when(p > 0)
        def _():
            by_kind(p - 1, relay)

    def each_block(first, last, run):
        @pl.loop(max(first, 1), min(last, 7))
        def _(g):
            run(g, FIRST)
            run(g, LAST)

        for g in (0, 7):
            if first <= g < last:
                run(g, WHOLE)

    def summed(g, part):
        for core in (0, 1):
            for i in (0, 1):
                slot = fin.at[i, place(z_of(g), core, part)]
                copy(slot, slot, s_x.at[0, 0, 0], r_fin.at[i, g, core, part % 2], sibling).wait_recv()
        slot = fin.at[2, place(z_of(g), 1 - c, part)]
        copy(slot, slot, s_x.at[0, 0, 0], r_sib.at[g, part % 2], sibling).wait_recv()

    heads = COLS // HD
    behind = lax.div(at_z(5) * (2 * ROWS) + HD - 1, HD)

    def leave(i):
        h = lax.rem(behind + i, heads)
        rows = pl.ds(pl.multiple_of(h * HD, HD), HD)
        return pltpu.make_async_copy(out.at[:, rows], qkv_out.at[:, rows], out_sem.at[i])

    def finish(i):
        h = lax.rem(behind + i, heads)
        rows = pl.ds(pl.multiple_of(h * HD, HD), HD)
        proj = (fin[0, rows].astype(jnp.float32) + fin[1, rows].astype(jnp.float32)) + fin[2, rows].astype(jnp.float32)
        proj = proj * columns[rows, 0:1]
        mean_sq = jnp.sum(proj * proj, axis=0, keepdims=True) / HD
        is_qk = x * heads + h < (QR + KR) // HD
        factor = jnp.where(is_qk, 1.0 / jnp.sqrt(mean_sq + norm_eps), 1.0 / math.sqrt(D))
        out[:, rows] = ((proj * factor).T * gain[rows].reshape(1, HD)).astype(jnp.bfloat16)
        leave(i).start()

    def sent(g, part):
        for i in range(7):
            send(g, part, i).wait_send()

    def sent_before():
        for store in stores():
            store.wait()
        for d in (1, 2, 3):
            sq_copy(d, x).wait_send()
            near_copy(d, y).wait_send()
        for d in range(1, NZ):
            far_copy(d).wait_send()
        swap(c).wait_send()
        tok_out.wait_send()
        for s in SIGNS:
            for hop in (1, 2):
                ay(hop, s).wait_send()
            for k in range(1, 5):
                bz(k, s).wait_send()
                for j in range(4):
                    az(k, s, j).wait_send()
            for dz in (0, 1, -1, 2, -2, 3, -3, 4):
                for hop in (1, 2):
                    by(dz, hop, s).wait_send()
        each_block(0, 6, sent)

    each_block(0, 6, summed)
    pl.loop(0, 6)(finish)
    relay([(7, WHOLE)])
    sent_before()
    each_block(6, 8, summed)
    pl.loop(6, heads)(finish)
    each_block(6, 8, sent)

    @pl.loop(0, heads)
    def _(i):
        leave(i).wait()


def hand_over_kernel(*refs):
    results, outputs, held, load_sem, store_sem = refs[0:4], refs[4:8], refs[8:12], refs[12], refs[13]
    blocks = []
    for i in range(4):
        size = results[i].shape[0] // 5 if i < 3 else results[i].shape[0] // 4
        blocks += [(i, n, pl.ds(n * size, size)) for n in range(5 if i < 3 else 4)]
    loads = [pltpu.make_async_copy(results[i].at[r], held[i].at[r], load_sem.at[i, n]) for i, n, r in blocks]
    stores = [pltpu.make_async_copy(held[i].at[r], outputs[i].at[r], store_sem.at[i, n]) for i, n, r in blocks]
    for load in loads:
        load.start()
    for load, store in zip(loads, stores):
        load.wait()
        store.start()
    for store in stores:
        store.wait()


def hand_over(*arrays):
    return pl.pallas_call(
        hand_over_kernel,
        out_shape=[jax.ShapeDtypeStruct(a.shape, a.dtype) for a in arrays],
        in_specs=[pl.BlockSpec(memory_space=pl.ANY)] * 4,
        out_specs=[pl.BlockSpec(memory_space=pl.ANY)] * 4,
        scratch_shapes=[pltpu.VMEM(a.shape, a.dtype) for a in arrays]
        + [pltpu.SemaphoreType.DMA((4, 5)), pltpu.SemaphoreType.DMA((4, 5))],
        compiler_params=pltpu.CompilerParams(vmem_limit_bytes=60 * 2**20),
    )(*arrays)


def body(tokens, qkv_weight, grad, adam_m, adam_v, head_gain):
    dma = pltpu.SemaphoreType.DMA
    anywhere = pl.BlockSpec(memory_space=pl.ANY)
    state = jax.ShapeDtypeStruct((ROWS, KS), jnp.float32)
    bf16 = jnp.bfloat16
    qkv, new_weight, new_m, new_v = pl.pallas_call(
        kernel,
        out_shape=(
            jax.ShapeDtypeStruct((TOK, COLS), bf16),
            state, state, state,
        ),
        in_specs=[pl.BlockSpec(memory_space=pltpu.HBM)] * 6,
        out_specs=[anywhere] * 4,
        scratch_shapes=[
            pltpu.VMEM((4, ROWS, KS), jnp.float32),
            pltpu.VMEM((NZ, NY, ROWS, KS), bf16),
            pltpu.VMEM((2, TOK, KS), bf16),
            pltpu.VMEM((8, NX, 2, ROWS, TOK), bf16),
            pltpu.VMEM((8, 2, ROWS, TOK), bf16),
            pltpu.VMEM((8, 2, ROWS, TOK), bf16),
            pltpu.VMEM((3, COLS, TOK), bf16),
            pltpu.VMEM((NX, ROWS, 128), jnp.float32),
            pltpu.VMEM((128, 128), jnp.float32),
            pltpu.VMEM((NY, 8, 128), jnp.float32),
            pltpu.VMEM((2, NZ, 8, 128), jnp.float32),
            pltpu.VMEM((COLS, 128), jnp.float32),
            pltpu.VMEM((COLS,), jnp.float32),
            pltpu.VMEM((TOK, COLS), bf16),
            dma((2, 2)), dma((2, 2)),
            dma((4, 2, 4)), dma((4, 2, 4)),
            dma((4, 2)), dma((4, 2)),
            dma((8, 2, 2)), dma((8, 2, 2)),
            dma((8, 2, 7)), dma((8, 2, 2)), dma((2, 8, 2, 2)), dma((8, 2)),
            dma((3,)), dma((3,)), dma((3,)), dma((3,)), dma((7,)), dma((7,)), dma((2,)), dma((1,)), dma((COLS // HD,)), dma((3,)), dma((ROWS // 16, 4)), dma((4,)),
        ],
        compiler_params=pltpu.CompilerParams(
            collective_id=0, has_side_effects=True, vmem_limit_bytes=60 * 2**20
        ),
        cost_estimate=pl.CostEstimate(
            flops=2 * 2 * TOK * KS * NZ * NY * ROWS, bytes_accessed=4 * 2**20, transcendentals=0
        ),
    )(tokens, qkv_weight, grad, adam_m, adam_v, head_gain)
    return hand_over(new_weight, new_m, new_v, qkv)


def solution(mesh):
    return jax.shard_map(
        body,
        mesh=mesh,
        in_specs=(
            P("dp", "hidden"),
            P("dp", "hidden"),
            P("dp", "hidden"),
            P("dp", "hidden"),
            P("dp", "hidden"),
            P("hidden"),
        ),
        out_specs=(P("dp", "hidden"), P("dp", "hidden"), P("dp", "hidden"), P("dp", "hidden")),
        check_vma=False,
    )
```
